512 devices in a mesh: dp: 64 (over x, z_hi, y), tensor: 8 (over z_lo, core).
Axes of the slice: x: 4, y: 4, z: 16 (z_hi: 4, z_lo: 4; z = z_hi * 4 + z_lo), core: 2. Of those that a mesh axis runs over, the one named last changes fastest.
Arguments:
- tokens: bfloat16 [1280, 6144], P('dp', 'tensor'), may hold values from -6 to 6
- route_ids: int32 [1280, 2], replicated, may hold values from 0 to 3, all different within a row
- route_probs: bfloat16 [1280, 2], replicated, may hold values from 0.099609375 to 1
- w_gate: bfloat16 [4, 6144, 8192], P(None, 'tensor', 'dp'), may hold values from -0.078125 to 0.078125
- w_up: bfloat16 [4, 6144, 8192], P(None, 'tensor', 'dp'), may hold values from -0.078125 to 0.078125
- w_down: bfloat16 [4, 8192, 6144], P(None, 'dp', 'tensor'), may hold values from -0.0625 to 0.0625
Outputs:
- mixed_out: bfloat16 [1280, 6144], P('dp', 'tensor')
The draws below stay inside these ranges and needn't reach their ends.
Inputs may be any that keep to these rules, and one draw needn't show every extreme that they name: `route_ids`: each row names 2 different experts, and every expert is named by some row.
All inputs are finite; a program needn't handle non-finite values.
Results may differ from the reference program's by a relative error of at most 0.0049.
Values may be sent and summed in bfloat16 or wider, within the bound.
A program may use at most 64 MiB of HBM per device.

```python
import jax
import jax.numpy as jnp
from jax import lax

D = 6144
FF = 8192
EXPERTS = 4
TOPK = 2
TOKENS = 1280


def block_levels(own_key, extent, split, low, high):
    factor_of, own = 1.0, jax.random.fold_in(own_key, 6)
    for dim, shards_of in split:
        draws = jnp.exp(jax.random.uniform(jax.random.fold_in(own, dim), (shards_of,), jnp.float32, low / len(split), high / len(split)))
        factor_of = factor_of * jnp.repeat(draws, extent[dim] // shards_of).reshape([-1 if axis == dim else 1 for axis in range(len(extent))])
    return factor_of


def different_ones(stream_key, rows, number_of, top, lift):
    order = jax.random.permutation(jax.random.fold_in(stream_key, 1), number_of)
    favour = order
    for power in range(3):
        favour = favour * favour // number_of
    favour = favour * lift // number_of
    chance = jax.random.randint(jax.random.fold_in(stream_key, 2), (rows, number_of), 0, 4096) + favour
    fixed_rows = jax.random.permutation(jax.random.fold_in(stream_key, 3), rows)[jnp.arange(number_of) % rows]
    chance = jnp.where(jnp.arange(rows)[:, None] == fixed_rows[None, :], 1 << 14, chance)
    score = chance * number_of + jnp.arange(number_of)
    return lax.top_k(score.astype(jnp.int32), top)[1].astype(jnp.int32)


def noise(key, shape, width, most, split=(), kind=jnp.bfloat16):
    values = jax.random.normal(key, shape, jnp.float32) * width
    if len(split) > 0:
        values = block_levels(key, shape, split, -0.22, 0.18) * values
    return jnp.clip(values, min=-most, max=most).astype(kind)


def setup_inputs(seed: int = 0) -> dict:
    keys = jax.random.split(jax.random.key(seed), 7)
    tokens = noise(keys[0], (TOKENS, D), 1.0, 6.0, ((0, 64), (1, 8)))
    route_ids = different_ones(keys[1], TOKENS, EXPERTS, TOPK, 8192)
    route_probs = jnp.clip(jax.random.uniform(keys[2], (TOKENS, TOPK), jnp.float32, 0.099609375, 1.0), 0.099609375, 1.0).astype(jnp.bfloat16)
    w_gate = noise(keys[3], (EXPERTS, D, FF), D ** -0.5, 0.078125, ((1, 8), (2, 64)))
    w_up = noise(keys[4], (EXPERTS, D, FF), D ** -0.5, 0.078125, ((1, 8), (2, 64)))
    w_down = noise(keys[5], (EXPERTS, FF, D), FF ** -0.5, 0.0625, ((1, 64), (2, 8)))
    return dict(tokens=tokens, route_ids=route_ids, route_probs=route_probs, w_gate=w_gate, w_up=w_up, w_down=w_down)


def reference(tokens, route_ids, route_probs, w_gate, w_up, w_down):
    route_weight = route_probs.astype(jnp.float32)
    mixed_sum = jnp.zeros((TOKENS, D), jnp.float32)
    for expert in range(EXPERTS):
        chosen = jnp.sum(jnp.where(route_ids == expert, route_weight, 0.0), axis=1)
        gate_sum = jnp.dot(tokens, w_gate[expert], preferred_element_type=jnp.float32)
        up_sum = jnp.dot(tokens, w_up[expert], preferred_element_type=jnp.float32)
        hidden = (gate_sum * jax.nn.sigmoid(gate_sum) * up_sum).astype(jnp.bfloat16)
        expert_out = jnp.dot(hidden, w_down[expert], preferred_element_type=jnp.float32)
        mixed_sum = mixed_sum + chosen[:, None] * expert_out
    return mixed_sum.astype(jnp.bfloat16)
```

```python
import jax
import jax.numpy as jnp
from jax import lax
from jax.experimental import pallas as pl
from jax.experimental.pallas import tpu as pltpu
from jax.sharding import Mesh
from jax.sharding import PartitionSpec as P

MESH = pl.DeviceIdType.MESH
F32, BF16 = jnp.float32, jnp.bfloat16
X, H, Y, L, C = "x", "zh", "y", "zl", "c"
DP = (X, H, Y)
TENSOR = (L, C)
EXPERTS = 4
HALF = 384
ROWS = 80
SHARE = 160


def kernel(
    tok_ref, ids_ref, probs_ref, wg_ref, wu_ref, wd_ref, out_ref,
    wcat, wdown, packed, unpacked, tok_a, tok_b,
    core_out, core_in, lane_out, lane_in, own, hid,
    part_a, part_b, send_a, send_b,
    in1_a, in1_b, in2_a, in2_b, in3,
    sum_a, sum_b, mixed, zsum,
    w_sem, ss, rs,
):
    x, h, y, l, c = (lax.axis_index(a) for a in (X, H, Y, L, C))
    place = {X: x, H: h, Y: y, L: l, C: c}
    pair = 1 - c

    loads = []
    for e in range(EXPERTS):
        loads.append((wg_ref.at[e], wcat.at[:, pl.ds(e * 256, 128)]))
        loads.append((wu_ref.at[e], wcat.at[:, pl.ds(e * 256 + 128, 128)]))
    for e in range(EXPERTS):
        loads.append((wd_ref.at[e], wdown.at[pl.ds(e * 128, 128), :]))
    loads = [pltpu.make_async_copy(s, d, w_sem.at[i]) for i, (s, d) in enumerate(loads)]
    for load in loads:
        load.start()

    def step(axis, by):
        return {axis: lax.rem(place[axis] + by, 4)}

    barrier = pltpu.get_barrier_semaphore()
    partners = [step(a, by) for a in (X, Y, H) for by in (1, 3)]
    partners += [step(L, by) for by in (1, 2, 3)] + [{C: pair}]
    for other in partners:
        pl.semaphore_signal(barrier, inc=1, device_id=other, device_id_type=MESH)
    pl.semaphore_wait(barrier, len(partners))

    sent = []

    def copy(src, dst, i, to):
        return pltpu.make_async_remote_copy(
            src_ref=src, dst_ref=dst, send_sem=ss.at[i], recv_sem=rs.at[i],
            device_id=to, device_id_type=MESH,
        )

    def send(src, dst, i, to):
        one = copy(src, dst, i, to)
        one.start()
        sent.append(one)

    def arrived(dst, i):
        copy(dst, dst, i, {C: pair}).wait_recv()

    class Gather:
        def __init__(self, axis, base, block, half):
            self.axis, self.base, self.block, self.half = axis, base, block, half
            me = place[axis]
            self.me, self.opp = me, lax.rem(me + 2, 4)
            self.right, self.left = lax.rem(me + 1, 4), lax.rem(me + 3, 4)

        def start(self):
            send(self.block(self.me), self.block(self.me), self.base, {self.axis: self.right})
            send(self.block(self.me), self.block(self.me), self.base + 1, {self.axis: self.left})

        def forward(self):
            arrived(self.block(self.left), self.base)
            send(self.half(self.left, 0), self.half(self.left, 0), self.base + 2, {self.axis: self.right})
            arrived(self.block(self.right), self.base + 1)
            send(self.half(self.right, 1), self.half(self.right, 1), self.base + 3, {self.axis: self.left})

        def finish(self):
            arrived(self.half(self.opp, 0), self.base + 2)
            arrived(self.half(self.opp, 1), self.base + 3)

    class Reduce:
        def __init__(self, axis, base, term, out, landing, kind):
            self.axis, self.base, self.term, self.out = axis, base, term, out
            self.landing, self.kind = landing, kind
            me = place[axis]
            self.me, self.opp = me, lax.rem(me + 2, 4)
            self.right, self.left = lax.rem(me + 1, 4), lax.rem(me + 3, 4)

        def start(self):
            to_right, to_left = {self.axis: self.right}, {self.axis: self.left}
            land, b = self.landing, self.base
            send(self.out(self.opp, 0), land(0, 0), b, to_right)
            send(self.out(self.opp, 1), land(0, 1), b + 1, to_left)
            send(self.out(self.right, 1), land(1, 1), b + 2, to_right)
            send(self.out(self.left, 0), land(2, 0), b + 3, to_left)

        def forward(self):
            to_right, to_left = {self.axis: self.right}, {self.axis: self.left}
            land, b = self.landing, self.base
            arrived(land(0, 0), b)
            land(3, 0)[...] = (self.term(self.right, 0)[...] + land(0, 0)[...].astype(F32)).astype(self.kind)
            send(land(3, 0), land(1, 0), b + 4, to_right)
            arrived(land(0, 1), b + 1)
            land(3, 1)[...] = (self.term(self.left, 1)[...] + land(0, 1)[...].astype(F32)).astype(self.kind)
            send(land(3, 1), land(2, 1), b + 5, to_left)

        def finish(self, half):
            land, b = self.landing, self.base
            if half == 0:
                arrived(land(2, 0), b + 3)
                arrived(land(1, 0), b + 4)
            else:
                arrived(land(1, 1), b + 2)
                arrived(land(2, 1), b + 5)
            return self.term(self.me, half)[...] + land(1, half)[...].astype(F32) + land(2, half)[...].astype(F32)

    mine = tok_ref[...].astype(F32)
    tail = [mine[16:20, 256 * j : 256 * (j + 1)] for j in range(3)]
    tail = jnp.concatenate([*tail, jnp.zeros((4, 256), F32)], axis=0)
    packed[h, 0] = mine[0:16, 0:512].astype(BF16)
    packed[h, 1] = jnp.concatenate([mine[0:16, 512:768], tail], axis=1).astype(BF16)
    over_z = Gather(H, 0, lambda i: packed.at[i], lambda i, p: packed.at[i, p])
    over_z.start()
    over_z.forward()
    over_z.finish()
    for i in range(4):
        unpacked[20 * i : 20 * i + 16, 0:512] = packed[i, 0].astype(F32)
        rest = packed[i, 1].astype(F32)
        unpacked[20 * i : 20 * i + 16, 512:768] = rest[:, 0:256]
        for j in range(3):
            unpacked[20 * i + 16 : 20 * i + 20, 256 * j : 256 * (j + 1)] = rest[4 * j : 4 * j + 4, 256:512]
    tok_a[y, x] = unpacked[:, 0:HALF].astype(BF16)
    tok_b[x, y] = unpacked[:, HALF:768].astype(BF16)

    rows_of = ((0, 48), (48, 32))
    first_a = Gather(X, 4, lambda i: tok_a.at[y, i], lambda i, p: tok_a.at[y, i, pl.ds(*rows_of[p]), :])
    first_b = Gather(Y, 8, lambda i: tok_b.at[x, i], lambda i, p: tok_b.at[x, i, pl.ds(*rows_of[p]), :])
    second_a = Gather(Y, 12, lambda i: tok_a.at[i], lambda i, p: tok_a.at[i, pl.ds(2 * p, 2)])
    second_b = Gather(X, 16, lambda i: tok_b.at[i], lambda i, p: tok_b.at[i, pl.ds(2 * p, 2)])
    for a, b in ((first_a, first_b), (second_a, second_b)):
        a.start()
        b.start()
        a.forward()
        b.forward()
        a.finish()
        b.finish()

    for load in loads:
        load.wait()

    def terms(i, core):
        left = jnp.concatenate([tok_a[2 * core, i], tok_a[2 * core + 1, i]], axis=0)
        right = tok_b[i, pl.ds(2 * core, 2)].reshape(SHARE, HALF)
        block = jnp.concatenate([left, right], axis=1)
        ids = ids_ref[i, core]
        picked = [None, None]
        for e in range(EXPERTS):
            both = jnp.dot(block, wcat[:, 256 * e : 256 * (e + 1)], preferred_element_type=F32)
            for k in range(2):
                picked[k] = both if e == 0 else jnp.where(ids[:, k : k + 1] == e, both, picked[k])
        return picked

    def for_pair(d, carry):
        i = lax.rem(l + d, 4)
        for k, value in enumerate(terms(i, pair)):
            core_out[i, :, 256 * k : 256 * (k + 1)] = value
        copy(core_out.at[i], core_in.at[i], 20 + d, {C: pair}).start()
        return carry

    def for_others(d, carry):
        i = lax.rem(l + d, 4)
        picked = terms(i, c)
        arrived(core_in.at[i], 20 + d)
        for k, value in enumerate(picked):
            at = slice(256 * k, 256 * (k + 1))
            lane_out[i, :, at] = (value + core_in[i, :, at]).astype(BF16)
        copy(lane_out.at[i], lane_in.at[d - 1], 24 + d, {L: i}).start()
        return carry

    lax.fori_loop(1, 4, for_pair, 0)
    for k, value in enumerate(terms(l, pair)):
        core_out[l, :, 256 * k : 256 * (k + 1)] = value
    copy(core_out.at[l], core_in.at[l], 20, {C: pair}).start()
    lax.fori_loop(1, 4, for_others, 0)
    picked = terms(l, c)
    arrived(core_in.at[l], 20)
    for k, value in enumerate(picked):
        at = slice(256 * k, 256 * (k + 1))
        own[:, at] = value + core_in[l, :, at]
    for d in (1, 2, 3):
        arrived(lane_in.at[d - 1], 24 + d)

    for k in range(2):
        at = slice(256 * k, 256 * (k + 1))
        total = own[:, at]
        for d in range(3):
            total = total + lane_in[d, :, at].astype(F32)
        gate, up = total[:, :128], total[:, 128:]
        weight = probs_ref[l, c][:, k : k + 1]
        hid[l, c, :, 128 * k : 128 * (k + 1)] = (gate / (1.0 + jnp.exp(-gate)) * up * weight).astype(BF16)

    mine = hid.at[l, c]
    send(mine, mine, 28, {C: pair})
    for d in (1, 2, 3):
        send(mine, mine, 28 + d, step(L, d))

    def second(i, core):
        ids = ids_ref[i, core]
        one, two = hid[i, core, :, 0:128], hid[i, core, :, 128:256]
        one, two = one.astype(F32), two.astype(F32)
        spread = []
        for e in range(EXPERTS):
            here = jnp.where(ids[:, 1:2] == e, two, 0.0)
            spread.append(jnp.where(ids[:, 0:1] == e, one, here).astype(BF16))
        spread = jnp.concatenate(spread, axis=1)
        result = jnp.dot(spread, wdown[...], preferred_element_type=F32)
        for j in range(2):
            piece = result[ROWS * j : ROWS * (j + 1)]
            part_a[i, 2 * core + j] = piece[:, :HALF]
            part_b[2 * core + j, i] = piece[:, HALF:]
            send_a[i, 2 * core + j] = piece[:, :HALF].astype(BF16)
            send_b[2 * core + j, i] = piece[:, HALF:].astype(BF16)

    second(l, c)

    def from_others(d, carry):
        i = lax.rem(l + 4 - d, 4)
        arrived(hid.at[i, c], 28 + d)
        copy(hid.at[i, c], hid.at[i, c], 32 + d, {C: pair}).start()
        second(i, c)
        return carry

    lax.fori_loop(1, 4, from_others, 0)
    arrived(hid.at[l, pair], 28)
    second(l, pair)

    def from_pair(d, carry):
        i = lax.rem(l + 4 - d, 4)
        arrived(hid.at[i, pair], 32 + d)
        second(i, pair)
        return carry

    lax.fori_loop(1, 4, from_pair, 0)

    one_a = Reduce(
        X, 36, lambda i, p: part_a.at[i, pl.ds(2 * p, 2)], lambda i, p: send_a.at[i, pl.ds(2 * p, 2)],
        lambda s, p: in1_a.at[s, pl.ds(2 * p, 2)], BF16,
    )
    one_b = Reduce(
        Y, 42, lambda i, p: part_b.at[i, pl.ds(2 * p, 2)], lambda i, p: send_b.at[i, pl.ds(2 * p, 2)],
        lambda s, p: in1_b.at[s, pl.ds(2 * p, 2)], BF16,
    )
    two_a = Reduce(
        Y, 48, lambda i, p: sum_a.at[i, pl.ds(40 * p, 40)], lambda i, p: sum_a.at[i, pl.ds(40 * p, 40)],
        lambda s, p: in2_a.at[s, pl.ds(40 * p, 40)], F32,
    )
    two_b = Reduce(
        X, 54, lambda i, p: sum_b.at[i, pl.ds(40 * p, 40)], lambda i, p: sum_b.at[i, pl.ds(40 * p, 40)],
        lambda s, p: in2_b.at[s, pl.ds(40 * p, 40)], F32,
    )
    three = Reduce(
        H, 60, lambda i, p: zsum.at[i, p], lambda i, p: zsum.at[i, p], lambda s, p: in3.at[s, p], F32,
    )
    one_a.start()
    one_b.start()
    one_a.forward()
    one_b.forward()
    for half in range(2):
        sum_a[2 * half : 2 * half + 2] = one_a.finish(half)
        sum_b[2 * half : 2 * half + 2] = one_b.finish(half)
    two_a.start()
    two_b.start()
    two_a.forward()
    two_b.forward()
    for half in range(2):
        mixed[40 * half : 40 * half + 40, 0:HALF] = two_a.finish(half)
        mixed[40 * half : 40 * half + 40, HALF:768] = two_b.finish(half)
    zsum[...] = jnp.zeros_like(zsum)
    for i in range(4):
        for p in range(2):
            zsum[i, p, 0:20] = mixed[20 * i : 20 * i + 20, HALF * p : HALF * (p + 1)]
    three.start()
    three.forward()
    for p in range(2):
        out_ref[:, HALF * p : HALF * (p + 1)] = three.finish(p)[0:20].astype(BF16)

    for one in sent:
        one.wait_send()

    def drain(d, carry):
        i = lax.rem(l + d, 4)
        copy(core_out.at[i], core_in.at[i], 20 + d, {C: pair}).wait_send()
        copy(lane_out.at[i], lane_in.at[d - 1], 24 + d, {L: i}).wait_send()
        back = lax.rem(l + 4 - d, 4)
        copy(hid.at[back, c], hid.at[back, c], 32 + d, {C: pair}).wait_send()
        return carry

    lax.fori_loop(1, 4, drain, 0)
    copy(core_out.at[l], core_in.at[l], 20, {C: pair}).wait_send()


def local(tokens, route_ids, route_probs, w_gate, w_up, w_down):
    def arranged(a):
        a = a.reshape(4, 4, 4, 20, 2).transpose(0, 2, 1, 3, 4)
        return a.reshape(4, 2, SHARE, 2)

    ids = arranged(route_ids)
    probs = arranged(route_probs.astype(F32))
    vmem = pl.BlockSpec(memory_space=pltpu.VMEM)
    hbm = pl.BlockSpec(memory_space=pl.ANY)
    return pl.pallas_call(
        kernel,
        out_shape=jax.ShapeDtypeStruct((20, 768), BF16),
        in_specs=[vmem, vmem, vmem, hbm, hbm, hbm],
        out_specs=vmem,
        scratch_shapes=[
            pltpu.VMEM((768, 1024), BF16),
            pltpu.VMEM((512, 768), BF16),
            pltpu.VMEM((4, 2, 16, 512), BF16),
            pltpu.VMEM((ROWS, 768), F32),
            pltpu.VMEM((4, 4, ROWS, HALF), BF16),
            pltpu.VMEM((4, 4, ROWS, HALF), BF16),
            pltpu.VMEM((4, SHARE, 512), F32),
            pltpu.VMEM((4, SHARE, 512), F32),
            pltpu.VMEM((4, SHARE, 512), BF16),
            pltpu.VMEM((3, SHARE, 512), BF16),
            pltpu.VMEM((SHARE, 512), F32),
            pltpu.VMEM((4, 2, SHARE, 256), BF16),
            pltpu.VMEM((4, 4, ROWS, HALF), F32),
            pltpu.VMEM((4, 4, ROWS, HALF), F32),
            pltpu.VMEM((4, 4, ROWS, HALF), BF16),
            pltpu.VMEM((4, 4, ROWS, HALF), BF16),
            pltpu.VMEM((4, 4, ROWS, HALF), BF16),
            pltpu.VMEM((4, 4, ROWS, HALF), BF16),
            pltpu.VMEM((4, ROWS, HALF), F32),
            pltpu.VMEM((4, ROWS, HALF), F32),
            pltpu.VMEM((4, 2, 24, HALF), F32),
            pltpu.VMEM((4, ROWS, HALF), F32),
            pltpu.VMEM((4, ROWS, HALF), F32),
            pltpu.VMEM((ROWS, 768), F32),
            pltpu.VMEM((4, 2, 24, HALF), F32),
            pltpu.SemaphoreType.DMA((12,)),
            pltpu.SemaphoreType.DMA((66,)),
            pltpu.SemaphoreType.DMA((66,)),
        ],
        compiler_params=pltpu.CompilerParams(
            collective_id=0, has_side_effects=True, vmem_limit_bytes=40 * 2**20
        ),
    )(tokens, ids, probs, w_gate, w_up, w_down)


def solution(mesh):
    torus = Mesh(mesh.devices.reshape(4, 4, 4, 4, 2), (X, H, Y, L, C))
    in_specs = (
        P(DP, TENSOR),
        P(),
        P(),
        P(None, TENSOR, DP),
        P(None, TENSOR, DP),
        P(None, DP, TENSOR),
    )
    return jax.shard_map(local, mesh=torus, in_specs=in_specs, out_specs=P(DP, TENSOR), check_vma=False)
```

```python
import jax
import jax.numpy as jnp
from jax import lax
from jax.experimental import pallas as pl
from jax.experimental.pallas import tpu as pltpu
from jax.sharding import Mesh
from jax.sharding import PartitionSpec as P

MESH = pl.DeviceIdType.MESH
F32, BF16 = jnp.float32, jnp.bfloat16
X, H, Y, L, C = "x", "zh", "y", "zl", "c"
DP = (X, H, Y)
TENSOR = (L, C)
EXPERTS = 4
WIDTH = 768
PIECE = 40
GROUP = 160


def kernel(
    tok_hbm, ids_hbm, probs_hbm, wg_ref, wu_ref, wd_ref, out_ref,
    tok_in, ids_in, probs_in, wcat, wdown, meta, packed, unpacked, tok,
    core_out, core_in, own, lane_out, lane_in, hid,
    part, send_part, in1, total, in2, z_own, z_out, z_in,
    w_sem, ss, rs,
):
    x, h, y, l, c = (lax.axis_index(a) for a in (X, H, Y, L, C))
    place = {X: x, H: h, Y: y, L: l, C: c}
    pair = 1 - c

    small = [(tok_hbm, tok_in), (ids_hbm, ids_in), (probs_hbm, probs_in)]
    loads = []
    for e in range(EXPERTS):
        loads.append((wg_ref.at[e], wcat.at[:, pl.ds(e * 256, 128)]))
        loads.append((wu_ref.at[e], wcat.at[:, pl.ds(e * 256 + 128, 128)]))
    for e in range(EXPERTS):
        loads.append((wd_ref.at[e], wdown.at[pl.ds(e * 128, 128), :]))
    loads = [pltpu.make_async_copy(s, d, w_sem.at[i]) for i, (s, d) in enumerate(small + loads)]
    for load in loads:
        load.start()

    def step(axis, by):
        return {axis: lax.rem(place[axis] + by, 4)}

    barrier = pltpu.get_barrier_semaphore()
    partners = [step(a, by) for a in (X, Y, H, L) for by in (1, 2, 3)] + [{C: pair}]
    for other in partners:
        pl.semaphore_signal(barrier, inc=1, device_id=other, device_id_type=MESH)

    sent, numbers = [], {}

    def copy(src, dst, key, to):
        i = numbers.setdefault(key, len(numbers))
        return pltpu.make_async_remote_copy(
            src_ref=src, dst_ref=dst, send_sem=ss.at[i], recv_sem=rs.at[i],
            device_id=to, device_id_type=MESH,
        )

    def send(src, dst, key, to):
        one = copy(src, dst, key, to)
        one.start()
        sent.append(one)

    def arrived(dst, key):
        copy(dst, dst, key, {C: pair}).wait_recv()

    def outer_place(r):
        return y + r * (x - y)

    def inner_place(r):
        return x + r * (y - x)

    def outer_to(r, o):
        return {X: x + r * (o - x), Y: o + r * (y - o)}

    def inner_to(r, i):
        return {X: i + r * (x - i), Y: y + r * (i - y)}

    def at(place_, d):
        return lax.rem(place_ + d, 4)

    for load in loads[:3]:
        load.wait()
    row = lax.broadcasted_iota(jnp.int32, (640, 1), 0)

    def count(value, size, most):
        return sum((value >= size * k).astype(jnp.int32) for k in range(1, most))

    xb = count(row, 320, 2)
    rest = row - 320 * xb
    part_of = count(rest, 160, 2)
    rest = rest - 160 * part_of
    yy = count(rest, PIECE, 4)
    rest = rest - PIECE * yy
    zz = count(rest, 20, 2)
    source = 320 * xb + (2 * part_of + zz) * 80 + yy * 20 + rest - 20 * zz
    order = (lax.broadcasted_iota(jnp.int32, (640, 640), 1) == source).astype(F32).astype(BF16)
    lines = jnp.concatenate([ids_in[...].astype(F32), probs_in[...].astype(F32), jnp.zeros((4, 1280), F32)], axis=0)
    lines = lines.astype(BF16)
    for two in range(2):
        columns = lax.dot_general(
            order, lines[:, 640 * two : 640 * (two + 1)], (((1,), (1,)), ((), ())), preferred_element_type=F32
        )
        for one in range(2):
            for yi in range(4):
                xi = 2 * two + one
                at0 = 320 * one + PIECE * yi
                meta[0, yi, xi] = columns[at0 : at0 + PIECE]
                meta[1, xi, yi] = columns[at0 + 160 : at0 + 160 + PIECE]

    def pack(block):
        tail = [block[16:20, 256 * j : 256 * (j + 1)] for j in range(3)]
        tail = jnp.concatenate([*tail, jnp.zeros((4, 256), F32)], axis=0)
        return jnp.concatenate([block[0:16], tail], axis=1).astype(BF16)

    packed[h] = pack(tok_in[...].astype(F32))
    pl.semaphore_wait(barrier, len(partners))

    for d in (1, 2, 3):
        send(packed.at[h], packed.at[h], ("z", d), step(H, d))
    for d in (1, 3, 2):
        arrived(packed.at[at(h, 4 - d)], ("z", d))
    for i in range(4):
        block = packed[i].astype(F32)
        unpacked[20 * i : 20 * i + 16] = block[:, 0:WIDTH]
        for j in range(3):
            unpacked[20 * i + 16 : 20 * i + 20, 256 * j : 256 * (j + 1)] = block[4 * j : 4 * j + 4, WIDTH:]
    for r in range(2):
        mine = tok.at[r, outer_place(r), inner_place(r)]
        mine[...] = unpacked[PIECE * r : PIECE * (r + 1)].astype(BF16)
        for d in (1, 3, 2):
            send(mine, mine, ("t", r, d), inner_to(r, at(inner_place(r), d)))
    for r in range(2):
        for d in (1, 3, 2):
            arrived(tok.at[r, outer_place(r), at(inner_place(r), 4 - d)], ("t", r, d))
        mine = tok.at[r, outer_place(r)]
        for d in (1, 3, 2):
            send(mine, mine, ("T", r, d), outer_to(r, at(outer_place(r), d)))
    for load in loads[3:]:
        load.wait()

    def terms(r, d):
        o = at(outer_place(r), d)
        block = tok[r, o].astype(F32).reshape(GROUP, WIDTH).astype(BF16)
        ids = meta[r, o].reshape(GROUP, 8)
        picked = [None, None]
        for e in range(EXPERTS):
            both = jnp.dot(block, wcat[:, 256 * e : 256 * (e + 1)], preferred_element_type=F32)
            for k in range(2):
                picked[k] = both if e == 0 else jnp.where(ids[:, k : k + 1] == float(e), both, picked[k])
        return picked

    def for_pair(d):
        for k, value in enumerate(terms(pair, d)):
            core_out[d, :, 256 * k : 256 * (k + 1)] = value
        send(core_out.at[d], core_in.at[d], ("c", d), {C: pair})

    def for_lanes(d):
        picked = terms(c, d)
        arrived(core_in.at[d], ("c", d))
        for k, value in enumerate(picked):
            cols = slice(256 * k, 256 * (k + 1))
            value = (value + core_in[d, :, cols]).reshape(4, PIECE, 256)
            own[d, :, :, cols] = value
            lane_out[d, :, :, cols] = value.astype(BF16)
        for j in (2, 3, 1):
            i = at(l, j)
            send(lane_out.at[d, i], lane_in.at[d, j - 1], ("l", d, j), {L: i})

    def hidden(d):
        o = at(outer_place(c), d)
        for j in (1, 3, 2):
            arrived(lane_in.at[d, j - 1], ("l", d, j))
        for k in range(2):
            cols = slice(256 * k, 256 * (k + 1))
            sums = own[d, l, :, cols]
            for j in range(3):
                sums = sums + lane_in[d, j, :, cols].astype(F32)
            gate, up = sums[:, :128], sums[:, 128:]
            weight = meta[c, o, l][:, 2 + k : 3 + k]
            hid[c, o, l, :, 128 * k : 128 * (k + 1)] = (gate / (1.0 + jnp.exp(-gate)) * up * weight).astype(BF16)
        mine = hid.at[c, o, l]
        for j in (2, 3, 1):
            send(mine, mine, ("h", d, j), step(L, j))
        send(mine, mine, ("p", d, 0), {C: pair})

    def forward(d):
        o = at(outer_place(c), d)
        for j in (1, 3, 2):
            piece = hid.at[c, o, at(l, 4 - j)]
            arrived(piece, ("h", d, j))
            send(piece, piece, ("p", d, j), {C: pair})

    def second(r, d, name):
        o = at(outer_place(r), d)
        if name == "pair":
            for j in range(4):
                arrived(hid.at[r, o, at(l, 4 - j)], ("p", d, j))
        ids = meta[r, o].reshape(GROUP, 8)
        units = hid[r, o].astype(F32).reshape(GROUP, 256)
        one, two = units[:, 0:128], units[:, 128:256]
        spread = []
        for e in range(EXPERTS):
            here = jnp.where(ids[:, 1:2] == float(e), two, 0.0)
            spread.append(jnp.where(ids[:, 0:1] == float(e), one, here).astype(BF16))
        spread = jnp.concatenate(spread, axis=1)
        result = jnp.dot(spread, wdown[...], preferred_element_type=F32).reshape(4, PIECE, WIDTH)
        if d == 0:
            part[r] = result
        else:
            send_part[r, d - 1] = result.astype(BF16)
            send(send_part.at[r, d - 1], in1.at[r, d - 1], ("s", name, d), outer_to(r, o))

    for_pair(0)
    for_lanes(0)
    for d in (1, 3, 2):
        for r in range(2):
            arrived(tok.at[r, at(outer_place(r), d)], ("T", r, 4 - d))
        for_pair(d)
        for_lanes(d)
        if d == 3:
            hidden(0)
    hidden(1)
    forward(0)
    hidden(3)
    forward(1)
    second(c, 1, "own")
    hidden(2)
    forward(3)
    second(pair, 1, "pair")
    second(c, 3, "own")
    second(pair, 3, "pair")
    forward(2)
    second(c, 2, "own")
    second(pair, 2, "pair")
    second(c, 0, "own")
    second(pair, 0, "pair")

    for name, r in (("own", c), ("pair", pair)):
        for d in (1, 3, 2):
            arrived(in1.at[r, d - 1], ("s", name, d))
        value = part[r]
        for d in range(3):
            value = value + in1[r, d].astype(F32)
        total[r] = value
        for d in (1, 3, 2):
            i = at(inner_place(r), d)
            send(total.at[r, i], in2.at[r, d - 1], ("S", name, d), inner_to(r, i))
    for name, r in (("own", c), ("pair", pair)):
        for d in (1, 3, 2):
            arrived(in2.at[r, d - 1], ("S", name, d))
    for r in range(2):
        value = total[r, inner_place(r)]
        for d in range(3):
            value = value + in2[r, d]
        for zi in range(2):
            block = value[20 * zi : 20 * (zi + 1)]
            z_own[2 * r + zi] = block
            z_out[2 * r + zi] = pack(block)
    for d in (2, 1, 3):
        i = at(h, d)
        send(z_out.at[i], z_in.at[d - 1], ("Z", d), {H: i})
    for d in (1, 3, 2):
        arrived(z_in.at[d - 1], ("Z", d))
    value = z_in[0].astype(F32) + z_in[1].astype(F32) + z_in[2].astype(F32)
    mine = z_own[h]
    bottom = jnp.concatenate([value[4 * j : 4 * j + 4, WIDTH:] for j in range(3)], axis=1)
    out_ref[...] = (mine + jnp.concatenate([value[:, :WIDTH], bottom], axis=0)).astype(BF16)

    for one in sent:
        one.wait_send()


def local(tokens, route_ids, route_probs, w_gate, w_up, w_down):
    hbm = pl.BlockSpec(memory_space=pl.ANY)
    return pl.pallas_call(
        kernel,
        out_shape=jax.ShapeDtypeStruct((20, WIDTH), BF16),
        in_specs=[hbm] * 6,
        out_specs=pl.BlockSpec(memory_space=pltpu.VMEM),
        scratch_shapes=[
            pltpu.VMEM((20, WIDTH), BF16),
            pltpu.VMEM((2, 1280), jnp.int32),
            pltpu.VMEM((2, 1280), BF16),
            pltpu.VMEM((WIDTH, 1024), BF16),
            pltpu.VMEM((512, WIDTH), BF16),
            pltpu.VMEM((2, 4, 4, PIECE, 8), F32),
            pltpu.VMEM((4, 16, 1024), BF16),
            pltpu.VMEM((80, WIDTH), F32),
            pltpu.VMEM((2, 4, 4, PIECE, WIDTH), BF16),
            pltpu.VMEM((4, GROUP, 512), F32),
            pltpu.VMEM((4, GROUP, 512), F32),
            pltpu.VMEM((4, 4, PIECE, 512), F32),
            pltpu.VMEM((4, 4, PIECE, 512), BF16),
            pltpu.VMEM((4, 3, PIECE, 512), BF16),
            pltpu.VMEM((2, 4, 4, PIECE, 256), BF16),
            pltpu.VMEM((2, 4, PIECE, WIDTH), F32),
            pltpu.VMEM((2, 3, 4, PIECE, WIDTH), BF16),
            pltpu.VMEM((2, 3, 4, PIECE, WIDTH), BF16),
            pltpu.VMEM((2, 4, PIECE, WIDTH), F32),
            pltpu.VMEM((2, 3, PIECE, WIDTH), F32),
            pltpu.VMEM((4, 20, WIDTH), F32),
            pltpu.VMEM((4, 16, 1024), BF16),
            pltpu.VMEM((3, 16, 1024), BF16),
            pltpu.SemaphoreType.DMA((15,)),
            pltpu.SemaphoreType.DMA((80,)),
            pltpu.SemaphoreType.DMA((80,)),
        ],
        compiler_params=pltpu.CompilerParams(
            collective_id=0, has_side_effects=True, vmem_limit_bytes=60 * 2**20
        ),
    )(tokens, route_ids.T, route_probs.T, w_gate, w_up, w_down)


def solution(mesh):
    torus = Mesh(mesh.devices.reshape(4, 4, 4, 4, 2), (X, H, Y, L, C))
    in_specs = (
        P(DP, TENSOR),
        P(),
        P(),
        P(None, TENSOR, DP),
        P(None, TENSOR, DP),
        P(None, DP, TENSOR),
    )
    return jax.shard_map(local, mesh=torus, in_specs=in_specs, out_specs=P(DP, TENSOR), check_vma=False)
```

```python
import jax
import jax.numpy as jnp
from jax import lax
from jax.experimental import pallas as pl
from jax.experimental.pallas import tpu as pltpu
from jax.sharding import Mesh
from jax.sharding import PartitionSpec as P

MESH = pl.DeviceIdType.MESH
F32, BF16 = jnp.float32, jnp.bfloat16
X, H, Y, L, C = "x", "zh", "y", "zl", "c"
DP = (X, H, Y)
TENSOR = (L, C)
EXPERTS = 4
WIDTH = 768
PIECE = 40
GROUP = 160


def kernel(
    tok_hbm, ids_hbm, probs_hbm, wg_ref, wu_ref, wd_ref, out_ref,
    tok_in, ids_in, probs_in, wcat, wdown, meta, packed, unpacked, tok,
    core_out, core_in, own, lane_out, lane_in, hid,
    part, send_part, in1, total, send_total, in2, z_own, z_out, z_in,
    w_sem, ss, rs,
):
    x, h, y, l, c = (lax.axis_index(a) for a in (X, H, Y, L, C))
    place = {X: x, H: h, Y: y, L: l, C: c}
    pair = 1 - c

    small = [(tok_hbm, tok_in), (ids_hbm, ids_in), (probs_hbm, probs_in)]
    loads = []
    for e in range(EXPERTS):
        loads.append((wg_ref.at[e], wcat.at[:, pl.ds(e * 256, 128)]))
        loads.append((wu_ref.at[e], wcat.at[:, pl.ds(e * 256 + 128, 128)]))
    for e in range(EXPERTS):
        loads.append((wd_ref.at[e], wdown.at[pl.ds(e * 128, 128), :]))
    loads = [pltpu.make_async_copy(s, d, w_sem.at[i]) for i, (s, d) in enumerate(small + loads)]
    for load in loads:
        load.start()

    def step(axis, by):
        return {axis: lax.rem(place[axis] + by, 4)}

    barrier = pltpu.get_barrier_semaphore()
    partners = [step(a, by) for a in (X, Y, H, L) for by in (1, 2, 3)] + [{C: pair}]
    for other in partners:
        pl.semaphore_signal(barrier, inc=1, device_id=other, device_id_type=MESH)

    sent, numbers = [], {}

    def copy(src, dst, key, to):
        i = numbers.setdefault(key, len(numbers))
        return pltpu.make_async_remote_copy(
            src_ref=src, dst_ref=dst, send_sem=ss.at[i], recv_sem=rs.at[i],
            device_id=to, device_id_type=MESH,
        )

    def send(src, dst, key, to):
        one = copy(src, dst, key, to)
        one.start()
        sent.append(one)

    def arrived(dst, key):
        copy(dst, dst, key, {C: pair}).wait_recv()

    def outer_place(r):
        return y + r * (x - y)

    def inner_place(r):
        return x + r * (y - x)

    def outer_to(r, o):
        return {X: x + r * (o - x), Y: o + r * (y - o)}

    def inner_to(r, i):
        return {X: i + r * (x - i), Y: y + r * (i - y)}

    def at(place_, d):
        return lax.rem(place_ + d, 4)

    for load in loads[:3]:
        load.wait()
    def pack(block):
        tail = [block[16:20, 256 * j : 256 * (j + 1)] for j in range(3)]
        tail = jnp.concatenate([*tail, jnp.zeros((4, 256), F32)], axis=0)
        return jnp.concatenate([block[0:16], tail], axis=1).astype(BF16)

    packed[h] = pack(tok_in[...].astype(F32))
    pl.semaphore_wait(barrier, len(partners))

    for d in (1, 2, 3):
        send(packed.at[h], packed.at[h], ("z", d), step(H, d))
    row = lax.broadcasted_iota(jnp.int32, (640, 1), 0)

    def count(value, size, most):
        return sum((value >= size * k).astype(jnp.int32) for k in range(1, most))

    xb = count(row, 320, 2)
    rest = row - 320 * xb
    part_of = count(rest, 160, 2)
    rest = rest - 160 * part_of
    yy = count(rest, PIECE, 4)
    rest = rest - PIECE * yy
    zz = count(rest, 20, 2)
    source = 320 * xb + (2 * part_of + zz) * 80 + yy * 20 + rest - 20 * zz
    order = (lax.broadcasted_iota(jnp.int32, (640, 640), 1) == source).astype(F32).astype(BF16)
    lines = jnp.concatenate([ids_in[...].astype(F32), probs_in[...].astype(F32), jnp.zeros((4, 1280), F32)], axis=0)
    lines = lines.astype(BF16)
    for two in range(2):
        columns = lax.dot_general(
            order, lines[:, 640 * two : 640 * (two + 1)], (((1,), (1,)), ((), ())), preferred_element_type=F32
        )
        for one in range(2):
            for yi in range(4):
                xi = 2 * two + one
                at0 = 320 * one + PIECE * yi
                meta[0, yi, xi] = columns[at0 : at0 + PIECE]
                meta[1, xi, yi] = columns[at0 + 160 : at0 + 160 + PIECE]

    for d in (1, 3, 2):
        arrived(packed.at[at(h, 4 - d)], ("z", d))
    for i in range(4):
        block = packed[i].astype(F32)
        unpacked[20 * i : 20 * i + 16] = block[:, 0:WIDTH]
        for j in range(3):
            unpacked[20 * i + 16 : 20 * i + 20, 256 * j : 256 * (j + 1)] = block[4 * j : 4 * j + 4, WIDTH:]
    def share_block(r, d, k):
        mine = tok.at[r, outer_place(r), at(inner_place(r), k)]
        send(mine, mine, ("T", r, d, k), outer_to(r, at(outer_place(r), d)))

    def share_group(r, d):
        mine = tok.at[r, outer_place(r)]
        send(mine, mine, ("T", r, d), outer_to(r, at(outer_place(r), d)))

    def group_arrived(d):
        for r in range(2):
            o = at(outer_place(r), d)
            if d == 2:
                arrived(tok.at[r, o], ("T", r, d))
            else:
                for k in (0, 3, 1, 2):
                    arrived(tok.at[r, o, at(inner_place(r), k)], ("T", r, 4 - d, k))

    for r in range(2):
        mine = tok.at[r, outer_place(r), inner_place(r)]
        mine[...] = unpacked[PIECE * r : PIECE * (r + 1)].astype(BF16)
        for d in (1, 3, 2):
            send(mine, mine, ("t", r, d), inner_to(r, at(inner_place(r), d)))
    for r in range(2):
        share_block(r, 1, 0)
        share_block(r, 3, 0)
    for d in (1, 3, 2):
        for r in range(2):
            arrived(tok.at[r, outer_place(r), at(inner_place(r), 4 - d)], ("t", r, d))
            share_block(r, 1, 4 - d)
            share_block(r, 3, 4 - d)
    for load in loads[3:]:
        load.wait()

    def terms(r, d):
        o = at(outer_place(r), d)
        block = tok[r, o].astype(F32).reshape(GROUP, WIDTH).astype(BF16)
        ids = meta[r, o].reshape(GROUP, 8)
        picked = [None, None]
        for e in range(EXPERTS):
            both = jnp.dot(block, wcat[:, 256 * e : 256 * (e + 1)], preferred_element_type=F32)
            for k in range(2):
                picked[k] = both if e == 0 else jnp.where(ids[:, k : k + 1] == float(e), both, picked[k])
        return picked

    def for_pair(d):
        for k, value in enumerate(terms(pair, d)):
            core_out[d, :, 256 * k : 256 * (k + 1)] = value
        send(core_out.at[d], core_in.at[d], ("c", d), {C: pair})

    def for_lanes(d):
        picked = terms(c, d)
        arrived(core_in.at[d], ("c", d))
        for k, value in enumerate(picked):
            cols = slice(256 * k, 256 * (k + 1))
            value = (value + core_in[d, :, cols]).reshape(4, PIECE, 256)
            own[d, :, :, cols] = value
            lane_out[d, :, :, cols] = value.astype(BF16)
        for j in (2, 3, 1):
            i = at(l, j)
            send(lane_out.at[d, i], lane_in.at[d, j - 1], ("l", d, j), {L: i})

    def hidden(d):
        o = at(outer_place(c), d)
        for j in (1, 3, 2):
            arrived(lane_in.at[d, j - 1], ("l", d, j))
        for k in range(2):
            cols = slice(256 * k, 256 * (k + 1))
            sums = own[d, l, :, cols]
            for j in range(3):
                sums = sums + lane_in[d, j, :, cols].astype(F32)
            gate, up = sums[:, :128], sums[:, 128:]
            weight = meta[c, o, l][:, 2 + k : 3 + k]
            hid[c, o, l, :, 128 * k : 128 * (k + 1)] = (gate / (1.0 + jnp.exp(-gate)) * up * weight).astype(BF16)
        mine = hid.at[c, o, l]
        for j in (2, 3, 1):
            send(mine, mine, ("h", d, j), step(L, j))
        send(mine, mine, ("p", d, 0), {C: pair})

    def forward(d):
        o = at(outer_place(c), d)
        for j in (1, 3, 2):
            piece = hid.at[c, o, at(l, 4 - j)]
            arrived(piece, ("h", d, j))
            send(piece, piece, ("p", d, j), {C: pair})

    def second(r, d, name):
        o = at(outer_place(r), d)
        if name == "pair":
            for j in range(4):
                arrived(hid.at[r, o, at(l, 4 - j)], ("p", d, j))
        ids = meta[r, o].reshape(GROUP, 8)
        units = hid[r, o].astype(F32).reshape(GROUP, 256)
        one, two = units[:, 0:128], units[:, 128:256]
        spread = []
        for e in range(EXPERTS):
            here = jnp.where(ids[:, 1:2] == float(e), two, 0.0)
            spread.append(jnp.where(ids[:, 0:1] == float(e), one, here).astype(BF16))
        spread = jnp.concatenate(spread, axis=1)
        result = jnp.dot(spread, wdown[...], preferred_element_type=F32).reshape(4, PIECE, WIDTH)
        if d == 0:
            part[r] = result
        else:
            send_part[r, d - 1] = result.astype(BF16)
            send(send_part.at[r, d - 1], in1.at[r, d - 1], ("s", name, d), outer_to(r, o))

    for_pair(0)
    for_lanes(0)
    group_arrived(1)
    group_arrived(3)
    share_group(0, 2)
    share_group(1, 2)
    for_pair(1)
    for_pair(3)
    for_lanes(1)
    for_lanes(3)
    group_arrived(2)
    for_pair(2)
    for_lanes(2)
    hidden(1)
    hidden(3)
    forward(1)
    second(c, 1, "own")
    forward(3)
    second(pair, 1, "pair")
    second(c, 3, "own")
    second(pair, 3, "pair")
    hidden(2)
    hidden(0)
    forward(2)
    second(c, 2, "own")
    second(pair, 2, "pair")
    forward(0)
    second(c, 0, "own")
    second(pair, 0, "pair")

    for name, r in (("own", c), ("pair", pair)):
        for d in (1, 3, 2):
            arrived(in1.at[r, d - 1], ("s", name, d))
        value = part[r]
        for d in range(3):
            value = value + in1[r, d].astype(F32)
        total[r] = value
        send_total[r] = value.astype(BF16)
        for d in (1, 3, 2):
            i = at(inner_place(r), d)
            send(send_total.at[r, i], in2.at[r, d - 1], ("S", name, d), inner_to(r, i))
    for name, r in (("own", c), ("pair", pair)):
        for d in (1, 3, 2):
            arrived(in2.at[r, d - 1], ("S", name, d))
    for r in range(2):
        value = total[r, inner_place(r)]
        for d in range(3):
            value = value + in2[r, d].astype(F32)
        for zi in range(2):
            block = value[20 * zi : 20 * (zi + 1)]
            z_own[2 * r + zi] = block
            z_out[2 * r + zi] = pack(block)
    for d in (1, 3, 2):
        i = at(h, d)
        send(z_out.at[i], z_in.at[d - 1], ("Z", d), {H: i})
    for d in (1, 3, 2):
        arrived(z_in.at[d - 1], ("Z", d))
    value = z_in[0].astype(F32) + z_in[1].astype(F32) + z_in[2].astype(F32)
    mine = z_own[h]
    bottom = jnp.concatenate([value[4 * j : 4 * j + 4, WIDTH:] for j in range(3)], axis=1)
    out_ref[...] = (mine + jnp.concatenate([value[:, :WIDTH], bottom], axis=0)).astype(BF16)

    for one in sent:
        one.wait_send()


def local(tokens, route_ids, route_probs, w_gate, w_up, w_down):
    hbm = pl.BlockSpec(memory_space=pl.ANY)
    return pl.pallas_call(
        kernel,
        out_shape=jax.ShapeDtypeStruct((20, WIDTH), BF16),
        in_specs=[hbm] * 6,
        out_specs=pl.BlockSpec(memory_space=pltpu.VMEM),
        scratch_shapes=[
            pltpu.VMEM((20, WIDTH), BF16),
            pltpu.VMEM((2, 1280), jnp.int32),
            pltpu.VMEM((2, 1280), BF16),
            pltpu.VMEM((WIDTH, 1024), BF16),
            pltpu.VMEM((512, WIDTH), BF16),
            pltpu.VMEM((2, 4, 4, PIECE, 8), F32),
            pltpu.VMEM((4, 16, 1024), BF16),
            pltpu.VMEM((80, WIDTH), F32),
            pltpu.VMEM((2, 4, 4, PIECE, WIDTH), BF16),
            pltpu.VMEM((4, GROUP, 512), F32),
            pltpu.VMEM((4, GROUP, 512), F32),
            pltpu.VMEM((4, 4, PIECE, 512), F32),
            pltpu.VMEM((4, 4, PIECE, 512), BF16),
            pltpu.VMEM((4, 3, PIECE, 512), BF16),
            pltpu.VMEM((2, 4, 4, PIECE, 256), BF16),
            pltpu.VMEM((2, 4, PIECE, WIDTH), F32),
            pltpu.VMEM((2, 3, 4, PIECE, WIDTH), BF16),
            pltpu.VMEM((2, 3, 4, PIECE, WIDTH), BF16),
            pltpu.VMEM((2, 4, PIECE, WIDTH), F32),
            pltpu.VMEM((2, 4, PIECE, WIDTH), BF16),
            pltpu.VMEM((2, 3, PIECE, WIDTH), BF16),
            pltpu.VMEM((4, 20, WIDTH), F32),
            pltpu.VMEM((4, 16, 1024), BF16),
            pltpu.VMEM((3, 16, 1024), BF16),
            pltpu.SemaphoreType.DMA((15,)),
            pltpu.SemaphoreType.DMA((96,)),
            pltpu.SemaphoreType.DMA((96,)),
        ],
        compiler_params=pltpu.CompilerParams(
            collective_id=0, has_side_effects=True, vmem_limit_bytes=60 * 2**20
        ),
    )(tokens, route_ids.T, route_probs.T, w_gate, w_up, w_down)


def solution(mesh):
    torus = Mesh(mesh.devices.reshape(4, 4, 4, 4, 2), (X, H, Y, L, C))
    in_specs = (
        P(DP, TENSOR),
        P(),
        P(),
        P(None, TENSOR, DP),
        P(None, TENSOR, DP),
        P(None, DP, TENSOR),
    )
    return jax.shard_map(local, mesh=torus, in_specs=in_specs, out_specs=P(DP, TENSOR), check_vma=False)
```

```python
import jax
import jax.numpy as jnp
from jax import lax
from jax.experimental import pallas as pl
from jax.experimental.pallas import tpu as pltpu
from jax.sharding import Mesh
from jax.sharding import PartitionSpec as P

MESH = pl.DeviceIdType.MESH
F32, BF16 = jnp.float32, jnp.bfloat16
X, H, Y, L, C = "x", "zh", "y", "zl", "c"
DP = (X, H, Y)
TENSOR = (L, C)
EXPERTS = 4
WIDTH = 768
PIECE = 40
GROUP = 160


def kernel(
    tok_hbm, ids_hbm, probs_hbm, wg_ref, wu_ref, wd_ref, out_ref,
    tok_in, ids_in, probs_in, wcat, wdown, meta, packed, unpacked, tok,
    core_out, core_in, own, lane_out, lane_in, hid,
    part, send_part, in1, total, send_total, in2, z_own, z_out, z_in,
    w_sem, ss, rs,
):
    x, h, y, l, c = (lax.axis_index(a) for a in (X, H, Y, L, C))
    place = {X: x, H: h, Y: y, L: l, C: c}
    pair = 1 - c

    small = [(tok_hbm, tok_in), (ids_hbm, ids_in), (probs_hbm, probs_in)]
    loads = []
    for e in range(EXPERTS):
        loads.append((wg_ref.at[e], wcat.at[:, pl.ds(e * 256, 128)]))
        loads.append((wu_ref.at[e], wcat.at[:, pl.ds(e * 256 + 128, 128)]))
    for e in range(EXPERTS):
        loads.append((wd_ref.at[e], wdown.at[pl.ds(e * 128, 128), :]))
    loads = [pltpu.make_async_copy(s, d, w_sem.at[i]) for i, (s, d) in enumerate(small + loads)]
    for load in loads:
        load.start()

    def step(axis, by):
        return {axis: lax.rem(place[axis] + by, 4)}

    barrier = pltpu.get_barrier_semaphore()
    partners = [step(a, by) for a in (X, Y, H, L) for by in (1, 2, 3)] + [{C: pair}]
    for other in partners:
        pl.semaphore_signal(barrier, inc=1, device_id=other, device_id_type=MESH)

    sent, numbers = [], {}

    def number(key):
        return numbers.setdefault(key, len(numbers))

    def copy(src, dst, key, to):
        i = number(key) if isinstance(key, tuple) else key
        return pltpu.make_async_remote_copy(
            src_ref=src, dst_ref=dst, send_sem=ss.at[i], recv_sem=rs.at[i],
            device_id=to, device_id_type=MESH,
        )

    def send(src, dst, key, to):
        one = copy(src, dst, key, to)
        one.start()
        sent.append(one)

    def arrived(dst, key):
        copy(dst, dst, key, {C: pair}).wait_recv()

    def outer_place(r):
        return y + r * (x - y)

    def inner_place(r):
        return x + r * (y - x)

    def outer_to(r, o):
        return {X: x + r * (o - x), Y: o + r * (y - o)}

    def inner_to(r, i):
        return {X: i + r * (x - i), Y: y + r * (i - y)}

    def at(place_, d):
        return lax.rem(place_ + d, 4)

    for load in loads[:3]:
        load.wait()
    def pack(block):
        tail = [block[16:20, 256 * j : 256 * (j + 1)] for j in range(3)]
        tail = jnp.concatenate([*tail, jnp.zeros((4, 256), F32)], axis=0)
        return jnp.concatenate([block[0:16], tail], axis=1).astype(BF16)

    packed[h] = pack(tok_in[...].astype(F32))
    pl.semaphore_wait(barrier, len(partners))

    for d in (1, 2, 3):
        send(packed.at[h], packed.at[h], ("z", d), step(H, d))
    row = lax.broadcasted_iota(jnp.int32, (640, 1), 0)

    def count(value, size, most):
        return sum((value >= size * k).astype(jnp.int32) for k in range(1, most))

    xb = count(row, 320, 2)
    rest = row - 320 * xb
    part_of = count(rest, 160, 2)
    rest = rest - 160 * part_of
    yy = count(rest, PIECE, 4)
    rest = rest - PIECE * yy
    zz = count(rest, 20, 2)
    source = 320 * xb + (2 * part_of + zz) * 80 + yy * 20 + rest - 20 * zz
    order = (lax.broadcasted_iota(jnp.int32, (640, 640), 1) == source).astype(F32).astype(BF16)
    lines = jnp.concatenate([ids_in[...].astype(F32), probs_in[...].astype(F32), jnp.zeros((4, 1280), F32)], axis=0)
    lines = lines.astype(BF16)
    for two in range(2):
        columns = lax.dot_general(
            order, lines[:, 640 * two : 640 * (two + 1)], (((1,), (1,)), ((), ())), preferred_element_type=F32
        )
        for one in range(2):
            for yi in range(4):
                xi = 2 * two + one
                at0 = 320 * one + PIECE * yi
                meta[0, yi, xi] = columns[at0 : at0 + PIECE]
                meta[1, xi, yi] = columns[at0 + 160 : at0 + 160 + PIECE]

    for d in (1, 3, 2):
        arrived(packed.at[at(h, 4 - d)], ("z", d))
    for i in range(4):
        block = packed[i].astype(F32)
        unpacked[20 * i : 20 * i + 16] = block[:, 0:WIDTH]
        for j in range(3):
            unpacked[20 * i + 16 : 20 * i + 20, 256 * j : 256 * (j + 1)] = block[4 * j : 4 * j + 4, WIDTH:]
    def share_block(r, d, k):
        mine = tok.at[r, outer_place(r), at(inner_place(r), k)]
        send(mine, mine, ("T", r, d, k), outer_to(r, at(outer_place(r), d)))

    def pass_on(k):
        for r in range(2):
            for d, blocks in ((3, (0, 1)), (1, (3, 2))):
                block = tok.at[r, at(outer_place(r), d), at(inner_place(r), k)]
                arrived(block, ("T", r, 4 - d, k))
                if k in blocks:
                    send(block, block, ("T", r, 2, k), outer_to(r, at(outer_place(r), 4 - d)))

    def opposite_arrived():
        for r in range(2):
            for k in range(4):
                arrived(tok.at[r, at(outer_place(r), 2), at(inner_place(r), k)], ("T", r, 2, k))

    for r in range(2):
        mine = tok.at[r, outer_place(r), inner_place(r)]
        mine[...] = unpacked[PIECE * r : PIECE * (r + 1)].astype(BF16)
        for d in (1, 3, 2):
            send(mine, mine, ("t", r, d), inner_to(r, at(inner_place(r), d)))
    for r in range(2):
        share_block(r, 1, 0)
        share_block(r, 3, 0)
    for d in (1, 3, 2):
        for r in range(2):
            arrived(tok.at[r, outer_place(r), at(inner_place(r), 4 - d)], ("t", r, d))
            share_block(r, 1, 4 - d)
            share_block(r, 3, 4 - d)
    for load in loads[3:]:
        load.wait()

    def terms(r, d):
        o = at(outer_place(r), d)
        block = tok[r, o].astype(F32).reshape(GROUP, WIDTH).astype(BF16)
        ids = meta[r, o].reshape(GROUP, 8)
        picked = [None, None]
        for e in range(EXPERTS):
            both = jnp.dot(block, wcat[:, 256 * e : 256 * (e + 1)], preferred_element_type=F32)
            for k in range(2):
                picked[k] = both if e == 0 else jnp.where(ids[:, k : k + 1] == float(e), both, picked[k])
        return picked

    def for_pair(d):
        for k, value in enumerate(terms(pair, d)):
            core_out[d, :, 256 * k : 256 * (k + 1)] = value
        send(core_out.at[d], core_in.at[d], ("c", d), {C: pair})

    def for_lanes(d):
        picked = terms(c, d)
        arrived(core_in.at[d], ("c", d))
        for k, value in enumerate(picked):
            cols = slice(256 * k, 256 * (k + 1))
            value = (value + core_in[d, :, cols]).reshape(4, PIECE, 256)
            own[d, :, :, cols] = value
            lane_out[d, :, :, cols] = value.astype(BF16)
        for j in (2, 3, 1):
            i = at(l, j)
            send(lane_out.at[d, i], lane_in.at[d, j - 1], ("l", d, j), {L: i})

    def hidden(d):
        o = at(outer_place(c), d)
        for j in (1, 3, 2):
            arrived(lane_in.at[d, j - 1], ("l", d, j))
        for k in range(2):
            cols = slice(256 * k, 256 * (k + 1))
            sums = own[d, l, :, cols]
            for j in range(3):
                sums = sums + lane_in[d, j, :, cols].astype(F32)
            gate, up = sums[:, :128], sums[:, 128:]
            weight = meta[c, o, l][:, 2 + k : 3 + k]
            hid[c, o, l, :, 128 * k : 128 * (k + 1)] = (gate / (1.0 + jnp.exp(-gate)) * up * weight).astype(BF16)
        mine = hid.at[c, o, l]
        for j in (2, 3, 1):
            send(mine, mine, ("h", d, j), step(L, j))
        send(mine, mine, ("p", d, 0), {C: pair})

    def forward(d):
        o = at(outer_place(c), d)
        for j in (1, 3, 2):
            piece = hid.at[c, o, at(l, 4 - j)]
            arrived(piece, ("h", d, j))
            send(piece, piece, ("p", d, j), {C: pair})

    def second(r, d, name):
        o = at(outer_place(r), d)
        if name == "pair":
            for j in range(4):
                arrived(hid.at[r, o, at(l, 4 - j)], ("p", d, j))
        ids = meta[r, o].reshape(GROUP, 8)
        units = hid[r, o].astype(F32).reshape(GROUP, 256)
        one, two = units[:, 0:128], units[:, 128:256]
        spread = []
        for e in range(EXPERTS):
            here = jnp.where(ids[:, 1:2] == float(e), two, 0.0)
            spread.append(jnp.where(ids[:, 0:1] == float(e), one, here).astype(BF16))
        spread = jnp.concatenate(spread, axis=1)
        result = jnp.dot(spread, wdown[...], preferred_element_type=F32).reshape(4, PIECE, WIDTH)
        if d == 0:
            part[r] = result
        else:
            send_part[r, d - 1] = result.astype(BF16)
            if d == 2:
                for k in (1, 3, 2, 0):
                    i = at(inner_place(r), k)
                    send(send_part.at[r, 1, i], in1.at[r, 1, i], ("s", name, d, k), outer_to(r, o))
            else:
                send(send_part.at[r, d - 1], in1.at[r, d - 1], ("s", name, d), outer_to(r, o))

    for_pair(0)
    pass_on(0)
    pass_on(3)
    for_lanes(0)
    pass_on(1)
    pass_on(2)
    for_pair(1)
    for_pair(3)
    for_lanes(1)
    for_lanes(3)
    opposite_arrived()
    for_pair(2)
    hidden(1)
    for_lanes(2)
    hidden(3)
    forward(1)
    second(c, 1, "own")
    forward(3)
    second(pair, 1, "pair")
    second(c, 3, "own")
    second(pair, 3, "pair")
    hidden(2)
    hidden(0)
    forward(2)
    second(c, 2, "own")
    second(pair, 2, "pair")
    forward(0)
    second(c, 0, "own")
    second(pair, 0, "pair")

    for name, r in (("own", c), ("pair", pair)):
        for d in (1, 3):
            arrived(in1.at[r, d - 1], ("s", name, d))
        for k in (1, 3, 2, 0):
            i = at(inner_place(r), k)
            arrived(in1.at[r, 1, i], ("s", name, 2, k))
            value = part[r, i]
            for d in range(3):
                value = value + in1[r, d, i].astype(F32)
            if k == 0:
                total[r] = value
            else:
                send_total[r, i] = value.astype(BF16)
                send(send_total.at[r, i], in2.at[r, k - 1], ("S", name, k), inner_to(r, i))
    from_zh = [number(("Z", d)) for d in range(4)][0]
    z_sends = []
    for name, r in (("own", c), ("pair", pair)):
        for d in (1, 3, 2):
            arrived(in2.at[r, d - 1], ("S", name, d))
        value = total[r]
        for d in range(3):
            value = value + in2[r, d].astype(F32)
        for zi in range(2):
            i = 2 * r + zi
            block = value[20 * zi : 20 * (zi + 1)]
            z_own[i] = block
            z_out[i] = pack(block)
            one = pltpu.make_async_remote_copy(
                src_ref=z_out.at[i], dst_ref=z_in.at[h], send_sem=ss.at[number(("Z", name, zi))],
                recv_sem=rs.at[from_zh + h], device_id={H: i}, device_id_type=MESH,
            )
            z_sends.append((i, one))
            pl.when(i != h)(one.start)
    for d in (1, 3, 2):
        arrived(z_in.at[at(h, d)], from_zh + at(h, d))
    value = z_in[at(h, 1)].astype(F32) + z_in[at(h, 2)].astype(F32) + z_in[at(h, 3)].astype(F32)
    mine = z_own[h]
    bottom = jnp.concatenate([value[4 * j : 4 * j + 4, WIDTH:] for j in range(3)], axis=1)
    out_ref[...] = (mine + jnp.concatenate([value[:, :WIDTH], bottom], axis=0)).astype(BF16)

    for one in sent:
        one.wait_send()
    for i, one in z_sends:
        pl.when(i != h)(one.wait_send)


def local(tokens, route_ids, route_probs, w_gate, w_up, w_down):
    hbm = pl.BlockSpec(memory_space=pl.ANY)
    return pl.pallas_call(
        kernel,
        out_shape=jax.ShapeDtypeStruct((20, WIDTH), BF16),
        in_specs=[hbm] * 6,
        out_specs=pl.BlockSpec(memory_space=pltpu.VMEM),
        scratch_shapes=[
            pltpu.VMEM((20, WIDTH), BF16),
            pltpu.VMEM((2, 1280), jnp.int32),
            pltpu.VMEM((2, 1280), BF16),
            pltpu.VMEM((WIDTH, 1024), BF16),
            pltpu.VMEM((512, WIDTH), BF16),
            pltpu.VMEM((2, 4, 4, PIECE, 8), F32),
            pltpu.VMEM((4, 16, 1024), BF16),
            pltpu.VMEM((80, WIDTH), F32),
            pltpu.VMEM((2, 4, 4, PIECE, WIDTH), BF16),
            pltpu.VMEM((4, GROUP, 512), F32),
            pltpu.VMEM((4, GROUP, 512), F32),
            pltpu.VMEM((4, 4, PIECE, 512), F32),
            pltpu.VMEM((4, 4, PIECE, 512), BF16),
            pltpu.VMEM((4, 3, PIECE, 512), BF16),
            pltpu.VMEM((2, 4, 4, PIECE, 256), BF16),
            pltpu.VMEM((2, 4, PIECE, WIDTH), F32),
            pltpu.VMEM((2, 3, 4, PIECE, WIDTH), BF16),
            pltpu.VMEM((2, 3, 4, PIECE, WIDTH), BF16),
            pltpu.VMEM((2, PIECE, WIDTH), F32),
            pltpu.VMEM((2, 4, PIECE, WIDTH), BF16),
            pltpu.VMEM((2, 3, PIECE, WIDTH), BF16),
            pltpu.VMEM((4, 20, WIDTH), F32),
            pltpu.VMEM((4, 16, 1024), BF16),
            pltpu.VMEM((4, 16, 1024), BF16),
            pltpu.SemaphoreType.DMA((15,)),
            pltpu.SemaphoreType.DMA((120,)),
            pltpu.SemaphoreType.DMA((120,)),
        ],
        compiler_params=pltpu.CompilerParams(
            collective_id=0, has_side_effects=True, vmem_limit_bytes=60 * 2**20
        ),
    )(tokens, route_ids.T, route_probs.T, w_gate, w_up, w_down)


def solution(mesh):
    torus = Mesh(mesh.devices.reshape(4, 4, 4, 4, 2), (X, H, Y, L, C))
    in_specs = (
        P(DP, TENSOR),
        P(),
        P(),
        P(None, TENSOR, DP),
        P(None, TENSOR, DP),
        P(None, DP, TENSOR),
    )
    return jax.shard_map(local, mesh=torus, in_specs=in_specs, out_specs=P(DP, TENSOR), check_vma=False)
```

```python
import jax
import jax.numpy as jnp
from jax import lax
from jax.experimental import pallas as pl
from jax.experimental.pallas import tpu as pltpu
from jax.sharding import Mesh
from jax.sharding import PartitionSpec as P

MESH = pl.DeviceIdType.MESH
F32, BF16 = jnp.float32, jnp.bfloat16
X, H, Y, L, C = "x", "zh", "y", "zl", "c"
DP = (X, H, Y)
TENSOR = (L, C)
EXPERTS = 4
WIDTH = 768
PIECE = 40
GROUP = 160


def kernel(
    tok_hbm, ids_hbm, probs_hbm, wg_ref, wu_ref, wd_ref, out_ref,
    tok_in, ids_in, probs_in, wcat, wdown, meta, packed, unpacked, tok,
    core_out, core_in, own, lane_out, lane_in, hid,
    part, send_part, in1, total, send_total, in2, z_own, z_out, z_in,
    w_sem, ss, rs,
):
    x, h, y, l, c = (lax.axis_index(a) for a in (X, H, Y, L, C))
    place = {X: x, H: h, Y: y, L: l, C: c}
    pair = 1 - c

    small = [(tok_hbm, tok_in), (ids_hbm, ids_in), (probs_hbm, probs_in)]
    loads = []
    for e in range(EXPERTS):
        loads.append((wg_ref.at[e], wcat.at[:, pl.ds(e * 256, 128)]))
        loads.append((wu_ref.at[e], wcat.at[:, pl.ds(e * 256 + 128, 128)]))
    for e in range(EXPERTS):
        loads.append((wd_ref.at[e], wdown.at[pl.ds(e * 128, 128), :]))
    loads = [pltpu.make_async_copy(s, d, w_sem.at[i]) for i, (s, d) in enumerate(small + loads)]
    for load in loads:
        load.start()

    def step(axis, by):
        return {axis: lax.rem(place[axis] + by, 4)}

    barrier = pltpu.get_barrier_semaphore()
    partners = [step(a, by) for a in (X, Y, H, L) for by in (1, 2, 3)] + [{C: pair}]
    for other in partners:
        pl.semaphore_signal(barrier, inc=1, device_id=other, device_id_type=MESH)

    sent, numbers = [], {}

    def number(key):
        return numbers.setdefault(key, len(numbers))

    def copy(src, dst, key, to):
        i = number(key) if isinstance(key, tuple) else key
        return pltpu.make_async_remote_copy(
            src_ref=src, dst_ref=dst, send_sem=ss.at[i], recv_sem=rs.at[i],
            device_id=to, device_id_type=MESH,
        )

    def send(src, dst, key, to):
        one = copy(src, dst, key, to)
        one.start()
        sent.append(one)

    def arrived(dst, key):
        copy(dst, dst, key, {C: pair}).wait_recv()

    def outer_place(r):
        return y + r * (x - y)

    def inner_place(r):
        return x + r * (y - x)

    def outer_to(r, o):
        return {X: x + r * (o - x), Y: o + r * (y - o)}

    def inner_to(r, i):
        return {X: i + r * (x - i), Y: y + r * (i - y)}

    def at(place_, d):
        return lax.rem(place_ + d, 4)

    for load in loads[:3]:
        load.wait()
    def pack(block):
        tail = [block[16:20, 256 * j : 256 * (j + 1)] for j in range(3)]
        tail = jnp.concatenate([*tail, jnp.zeros((4, 256), F32)], axis=0)
        return jnp.concatenate([block[0:16], tail], axis=1).astype(BF16)

    packed[h] = pack(tok_in[...].astype(F32))
    pl.semaphore_wait(barrier, len(partners))

    for d in (1, 2, 3):
        send(packed.at[h], packed.at[h], ("z", d), step(H, d))
    row = lax.broadcasted_iota(jnp.int32, (640, 1), 0)

    def count(value, size, most):
        return sum((value >= size * k).astype(jnp.int32) for k in range(1, most))

    xb = count(row, 320, 2)
    rest = row - 320 * xb
    part_of = count(rest, 160, 2)
    rest = rest - 160 * part_of
    yy = count(rest, PIECE, 4)
    rest = rest - PIECE * yy
    zz = count(rest, 20, 2)
    source = 320 * xb + (2 * part_of + zz) * 80 + yy * 20 + rest - 20 * zz
    order = (lax.broadcasted_iota(jnp.int32, (640, 640), 1) == source).astype(F32).astype(BF16)
    lines = jnp.concatenate([ids_in[...].astype(F32), probs_in[...].astype(F32), jnp.zeros((4, 1280), F32)], axis=0)
    lines = lines.astype(BF16)
    for two in range(2):
        columns = lax.dot_general(
            order, lines[:, 640 * two : 640 * (two + 1)], (((1,), (1,)), ((), ())), preferred_element_type=F32
        )
        for one in range(2):
            for yi in range(4):
                xi = 2 * two + one
                at0 = 320 * one + PIECE * yi
                meta[0, yi, xi] = columns[at0 : at0 + PIECE]
                meta[1, xi, yi] = columns[at0 + 160 : at0 + 160 + PIECE]

    for d in (1, 3, 2):
        arrived(packed.at[at(h, 4 - d)], ("z", d))
    for i in range(4):
        block = packed[i].astype(F32)
        unpacked[20 * i : 20 * i + 16] = block[:, 0:WIDTH]
        for j in range(3):
            unpacked[20 * i + 16 : 20 * i + 20, 256 * j : 256 * (j + 1)] = block[4 * j : 4 * j + 4, WIDTH:]
    def share_block(r, d, k):
        mine = tok.at[r, outer_place(r), at(inner_place(r), k)]
        send(mine, mine, ("T", r, d, k), outer_to(r, at(outer_place(r), d)))

    def pass_on(k):
        for r in range(2):
            for d, blocks in ((3, (0, 1)), (1, (3, 2))):
                block = tok.at[r, at(outer_place(r), d), at(inner_place(r), k)]
                arrived(block, ("T", r, 4 - d, k))
                if k in blocks:
                    send(block, block, ("T", r, 2, k), outer_to(r, at(outer_place(r), 4 - d)))

    def opposite_arrived():
        for r in range(2):
            for k in range(4):
                arrived(tok.at[r, at(outer_place(r), 2), at(inner_place(r), k)], ("T", r, 2, k))

    for r in range(2):
        mine = tok.at[r, outer_place(r), inner_place(r)]
        mine[...] = unpacked[PIECE * r : PIECE * (r + 1)].astype(BF16)
        for d in (1, 3, 2):
            send(mine, mine, ("t", r, d), inner_to(r, at(inner_place(r), d)))
    for r in range(2):
        share_block(r, 1, 0)
        share_block(r, 3, 0)
    for d in (1, 3, 2):
        for r in range(2):
            arrived(tok.at[r, outer_place(r), at(inner_place(r), 4 - d)], ("t", r, d))
            share_block(r, 1, 4 - d)
            share_block(r, 3, 4 - d)
    for load in loads[3:]:
        load.wait()

    def terms(r, d):
        o = at(outer_place(r), d)
        block = tok[r, o].astype(F32).reshape(GROUP, WIDTH).astype(BF16)
        ids = meta[r, o].reshape(GROUP, 8)
        picked = [None, None]
        for e in range(EXPERTS):
            both = jnp.dot(block, wcat[:, 256 * e : 256 * (e + 1)], preferred_element_type=F32)
            for k in range(2):
                picked[k] = both if e == 0 else jnp.where(ids[:, k : k + 1] == float(e), both, picked[k])
        return picked

    def for_pair(d):
        for k, value in enumerate(terms(pair, d)):
            core_out[d, :, 256 * k : 256 * (k + 1)] = value
        send(core_out.at[d], core_in.at[d], ("c", d), {C: pair})

    def for_lanes(d):
        picked = terms(c, d)
        arrived(core_in.at[d], ("c", d))
        for k, value in enumerate(picked):
            cols = slice(256 * k, 256 * (k + 1))
            value = (value + core_in[d, :, cols]).reshape(4, PIECE, 256)
            own[d, :, :, cols] = value
            lane_out[d, :, :, cols] = value.astype(BF16)
        for j in (2, 3, 1):
            i = at(l, j)
            send(lane_out.at[d, i], lane_in.at[d, j - 1], ("l", d, j), {L: i})

    def hidden(d):
        o = at(outer_place(c), d)
        for j in (1, 3, 2):
            arrived(lane_in.at[d, j - 1], ("l", d, j))
        for k in range(2):
            cols = slice(256 * k, 256 * (k + 1))
            sums = own[d, l, :, cols]
            for j in range(3):
                sums = sums + lane_in[d, j, :, cols].astype(F32)
            gate, up = sums[:, :128], sums[:, 128:]
            weight = meta[c, o, l][:, 2 + k : 3 + k]
            hid[c, o, l, :, 128 * k : 128 * (k + 1)] = (gate / (1.0 + jnp.exp(-gate)) * up * weight).astype(BF16)
        mine = hid.at[c, o, l]
        for j in (2, 3, 1):
            send(mine, mine, ("h", d, j), step(L, j))
        send(mine, mine, ("p", d, 0), {C: pair})

    def forward(d):
        o = at(outer_place(c), d)
        for j in (1, 3, 2):
            piece = hid.at[c, o, at(l, 4 - j)]
            arrived(piece, ("h", d, j))
            send(piece, piece, ("p", d, j), {C: pair})

    def second(r, d, name):
        o = at(outer_place(r), d)
        if name == "pair":
            for j in range(4):
                arrived(hid.at[r, o, at(l, 4 - j)], ("p", d, j))
        ids = meta[r, o].reshape(GROUP, 8)
        units = hid[r, o].astype(F32).reshape(GROUP, 256)
        one, two = units[:, 0:128], units[:, 128:256]
        spread = []
        for e in range(EXPERTS):
            here = jnp.where(ids[:, 1:2] == float(e), two, 0.0)
            spread.append(jnp.where(ids[:, 0:1] == float(e), one, here).astype(BF16))
        spread = jnp.concatenate(spread, axis=1)
        result = jnp.dot(spread, wdown[...], preferred_element_type=F32).reshape(4, PIECE, WIDTH)
        if d == 0:
            part[r] = result
        else:
            send_part[r, d - 1] = result.astype(BF16)
            if d == 2:
                for k in (1, 3, 2, 0):
                    i = at(inner_place(r), k)
                    send(send_part.at[r, 1, i], in1.at[r, 1, i], ("s", name, d, k), outer_to(r, o))
            else:
                send(send_part.at[r, d - 1], in1.at[r, d - 1], ("s", name, d), outer_to(r, o))

    for_pair(0)
    pass_on(0)
    pass_on(3)
    for_lanes(0)
    pass_on(1)
    pass_on(2)
    for_pair(1)
    for_pair(3)
    for_lanes(1)
    for_lanes(3)
    opposite_arrived()
    for_pair(2)
    hidden(1)
    for_lanes(2)
    hidden(3)
    forward(1)
    second(c, 1, "own")
    hidden(2)
    forward(3)
    second(pair, 1, "pair")
    hidden(0)
    second(c, 3, "own")
    forward(2)
    second(pair, 3, "pair")
    second(c, 2, "own")
    second(pair, 2, "pair")
    forward(0)
    second(c, 0, "own")
    second(pair, 0, "pair")

    for name, r in (("own", c), ("pair", pair)):
        for d in (1, 3):
            arrived(in1.at[r, d - 1], ("s", name, d))
        for k in (1, 3, 2, 0):
            i = at(inner_place(r), k)
            arrived(in1.at[r, 1, i], ("s", name, 2, k))
            value = part[r, i]
            for d in range(3):
                value = value + in1[r, d, i].astype(F32)
            if k == 0:
                total[r] = value
            else:
                send_total[r, i] = value.astype(BF16)
                send(send_total.at[r, i], in2.at[r, k - 1], ("S", name, k), inner_to(r, i))
    from_zh = [number(("Z", d)) for d in range(4)][0]
    z_sends = []
    for name, r in (("own", c), ("pair", pair)):
        for d in (1, 3, 2):
            arrived(in2.at[r, d - 1], ("S", name, d))
        value = total[r]
        for d in range(3):
            value = value + in2[r, d].astype(F32)
        for zi in range(2):
            i = 2 * r + zi
            block = value[20 * zi : 20 * (zi + 1)]
            z_own[i] = block
            z_out[i] = pack(block)
            one = pltpu.make_async_remote_copy(
                src_ref=z_out.at[i], dst_ref=z_in.at[h], send_sem=ss.at[number(("Z", name, zi))],
                recv_sem=rs.at[from_zh + h], device_id={H: i}, device_id_type=MESH,
            )
            z_sends.append((i, one))
            pl.when(i != h)(one.start)
    for d in (1, 3, 2):
        arrived(z_in.at[at(h, d)], from_zh + at(h, d))
    value = z_in[at(h, 1)].astype(F32) + z_in[at(h, 2)].astype(F32) + z_in[at(h, 3)].astype(F32)
    mine = z_own[h]
    bottom = jnp.concatenate([value[4 * j : 4 * j + 4, WIDTH:] for j in range(3)], axis=1)
    out_ref[...] = (mine + jnp.concatenate([value[:, :WIDTH], bottom], axis=0)).astype(BF16)

    for one in sent:
        one.wait_send()
    for i, one in z_sends:
        pl.when(i != h)(one.wait_send)


def local(tokens, route_ids, route_probs, w_gate, w_up, w_down):
    hbm = pl.BlockSpec(memory_space=pl.ANY)
    return pl.pallas_call(
        kernel,
        out_shape=jax.ShapeDtypeStruct((20, WIDTH), BF16),
        in_specs=[hbm] * 6,
        out_specs=pl.BlockSpec(memory_space=pltpu.VMEM),
        scratch_shapes=[
            pltpu.VMEM((20, WIDTH), BF16),
            pltpu.VMEM((2, 1280), jnp.int32),
            pltpu.VMEM((2, 1280), BF16),
            pltpu.VMEM((WIDTH, 1024), BF16),
            pltpu.VMEM((512, WIDTH), BF16),
            pltpu.VMEM((2, 4, 4, PIECE, 8), F32),
            pltpu.VMEM((4, 16, 1024), BF16),
            pltpu.VMEM((80, WIDTH), F32),
            pltpu.VMEM((2, 4, 4, PIECE, WIDTH), BF16),
            pltpu.VMEM((4, GROUP, 512), F32),
            pltpu.VMEM((4, GROUP, 512), F32),
            pltpu.VMEM((4, 4, PIECE, 512), F32),
            pltpu.VMEM((4, 4, PIECE, 512), BF16),
            pltpu.VMEM((4, 3, PIECE, 512), BF16),
            pltpu.VMEM((2, 4, 4, PIECE, 256), BF16),
            pltpu.VMEM((2, 4, PIECE, WIDTH), F32),
            pltpu.VMEM((2, 3, 4, PIECE, WIDTH), BF16),
            pltpu.VMEM((2, 3, 4, PIECE, WIDTH), BF16),
            pltpu.VMEM((2, PIECE, WIDTH), F32),
            pltpu.VMEM((2, 4, PIECE, WIDTH), BF16),
            pltpu.VMEM((2, 3, PIECE, WIDTH), BF16),
            pltpu.VMEM((4, 20, WIDTH), F32),
            pltpu.VMEM((4, 16, 1024), BF16),
            pltpu.VMEM((4, 16, 1024), BF16),
            pltpu.SemaphoreType.DMA((15,)),
            pltpu.SemaphoreType.DMA((120,)),
            pltpu.SemaphoreType.DMA((120,)),
        ],
        compiler_params=pltpu.CompilerParams(
            collective_id=0, has_side_effects=True, vmem_limit_bytes=60 * 2**20
        ),
    )(tokens, route_ids.T, route_probs.T, w_gate, w_up, w_down)


def solution(mesh):
    torus = Mesh(mesh.devices.reshape(4, 4, 4, 4, 2), (X, H, Y, L, C))
    in_specs = (
        P(DP, TENSOR),
        P(),
        P(),
        P(None, TENSOR, DP),
        P(None, TENSOR, DP),
        P(None, DP, TENSOR),
    )
    return jax.shard_map(local, mesh=torus, in_specs=in_specs, out_specs=P(DP, TENSOR), check_vma=False)
```

```python
import jax
import jax.numpy as jnp
from jax import lax
from jax.experimental import pallas as pl
from jax.experimental.pallas import tpu as pltpu
from jax.sharding import Mesh
from jax.sharding import PartitionSpec as P

MESH = pl.DeviceIdType.MESH
F32, BF16 = jnp.float32, jnp.bfloat16
X, H, Y, L, C = "x", "zh", "y", "zl", "c"
DP = (X, H, Y)
TENSOR = (L, C)
EXPERTS = 4
WIDTH = 768
PIECE = 40
GROUP = 160


def kernel(
    tok_hbm, ids_hbm, probs_hbm, wg_ref, wu_ref, wd_ref, out_ref,
    tok_in, ids_in, probs_in, wcat, wdown, meta, packed, unpacked, tok,
    core_out, core_in, own, lane_out, lane_in, hid,
    part, send_part, in1, total, send_total, in2, z_own, z_out, z_in,
    w_sem, ss, rs,
):
    x, h, y, l, c = (lax.axis_index(a) for a in (X, H, Y, L, C))
    place = {X: x, H: h, Y: y, L: l, C: c}
    pair = 1 - c

    small = [(tok_hbm, tok_in), (ids_hbm, ids_in), (probs_hbm, probs_in)]
    loads = []
    for e in range(EXPERTS):
        loads.append((wg_ref.at[e], wcat.at[:, pl.ds(e * 256, 128)]))
        loads.append((wu_ref.at[e], wcat.at[:, pl.ds(e * 256 + 128, 128)]))
    for e in range(EXPERTS):
        loads.append((wd_ref.at[e], wdown.at[pl.ds(e * 128, 128), :]))
    loads = [pltpu.make_async_copy(s, d, w_sem.at[i]) for i, (s, d) in enumerate(small + loads)]
    for load in loads:
        load.start()

    def step(axis, by):
        return {axis: lax.rem(place[axis] + by, 4)}

    barrier = pltpu.get_barrier_semaphore()
    partners = [step(a, by) for a in (X, Y, H, L) for by in (1, 2, 3)] + [{C: pair}]
    for other in partners:
        pl.semaphore_signal(barrier, inc=1, device_id=other, device_id_type=MESH)

    sent, numbers = [], {}

    def number(key):
        return numbers.setdefault(key, len(numbers))

    def copy(src, dst, key, to):
        i = number(key) if isinstance(key, tuple) else key
        return pltpu.make_async_remote_copy(
            src_ref=src, dst_ref=dst, send_sem=ss.at[i], recv_sem=rs.at[i],
            device_id=to, device_id_type=MESH,
        )

    def send(src, dst, key, to):
        one = copy(src, dst, key, to)
        one.start()
        sent.append(one)

    def arrived(dst, key):
        copy(dst, dst, key, {C: pair}).wait_recv()

    def outer_place(r):
        return y + r * (x - y)

    def inner_place(r):
        return x + r * (y - x)

    def outer_to(r, o):
        return {X: x + r * (o - x), Y: o + r * (y - o)}

    def inner_to(r, i):
        return {X: i + r * (x - i), Y: y + r * (i - y)}

    def at(place_, d):
        return lax.rem(place_ + d, 4)

    for load in loads[:3]:
        load.wait()
    def pack(block):
        tail = [block[16:20, 256 * j : 256 * (j + 1)] for j in range(3)]
        tail = jnp.concatenate([*tail, jnp.zeros((4, 256), F32)], axis=0)
        return jnp.concatenate([block[0:16], tail], axis=1).astype(BF16)

    packed[h] = pack(tok_in[...].astype(F32))
    pl.semaphore_wait(barrier, len(partners))

    for d in (1, 2, 3):
        send(packed.at[h], packed.at[h], ("z", d), step(H, d))
    row = lax.broadcasted_iota(jnp.int32, (640, 1), 0)

    def count(value, size, most):
        return sum((value >= size * k).astype(jnp.int32) for k in range(1, most))

    xb = count(row, 320, 2)
    rest = row - 320 * xb
    part_of = count(rest, 160, 2)
    rest = rest - 160 * part_of
    yy = count(rest, PIECE, 4)
    rest = rest - PIECE * yy
    zz = count(rest, 20, 2)
    source = 320 * xb + (2 * part_of + zz) * 80 + yy * 20 + rest - 20 * zz
    order = (lax.broadcasted_iota(jnp.int32, (640, 640), 1) == source).astype(F32).astype(BF16)
    lines = jnp.concatenate([ids_in[...].astype(F32), probs_in[...].astype(F32), jnp.zeros((4, 1280), F32)], axis=0)
    lines = lines.astype(BF16)
    for two in range(2):
        columns = lax.dot_general(
            order, lines[:, 640 * two : 640 * (two + 1)], (((1,), (1,)), ((), ())), preferred_element_type=F32
        )
        for one in range(2):
            for yi in range(4):
                xi = 2 * two + one
                at0 = 320 * one + PIECE * yi
                meta[0, yi, xi] = columns[at0 : at0 + PIECE]
                meta[1, xi, yi] = columns[at0 + 160 : at0 + 160 + PIECE]

    for d in (1, 3, 2):
        arrived(packed.at[at(h, 4 - d)], ("z", d))
    for i in range(4):
        block = packed[i].astype(F32)
        unpacked[20 * i : 20 * i + 16] = block[:, 0:WIDTH]
        for j in range(3):
            unpacked[20 * i + 16 : 20 * i + 20, 256 * j : 256 * (j + 1)] = block[4 * j : 4 * j + 4, WIDTH:]
    def share_block(r, d, k):
        mine = tok.at[r, outer_place(r), at(inner_place(r), k)]
        send(mine, mine, ("T", r, d, k), outer_to(r, at(outer_place(r), d)))

    def pass_on(k):
        for r in range(2):
            for d, blocks in ((3, (0, 1)), (1, (3, 2))):
                block = tok.at[r, at(outer_place(r), d), at(inner_place(r), k)]
                arrived(block, ("T", r, 4 - d, k))
                if k in blocks:
                    send(block, block, ("T", r, 2, k), outer_to(r, at(outer_place(r), 4 - d)))

    def opposite_arrived():
        for r in range(2):
            for k in range(4):
                arrived(tok.at[r, at(outer_place(r), 2), at(inner_place(r), k)], ("T", r, 2, k))

    for r in range(2):
        mine = tok.at[r, outer_place(r), inner_place(r)]
        mine[...] = unpacked[PIECE * r : PIECE * (r + 1)].astype(BF16)
        for d in (1, 3, 2):
            send(mine, mine, ("t", r, d), inner_to(r, at(inner_place(r), d)))
    for r in range(2):
        share_block(r, 1, 0)
        share_block(r, 3, 0)
    for d in (1, 3, 2):
        for r in range(2):
            arrived(tok.at[r, outer_place(r), at(inner_place(r), 4 - d)], ("t", r, d))
            share_block(r, 1, 4 - d)
            share_block(r, 3, 4 - d)
    for load in loads[3:]:
        load.wait()

    def terms(r, d):
        o = at(outer_place(r), d)
        block = tok[r, o].astype(F32).reshape(GROUP, WIDTH).astype(BF16)
        ids = meta[r, o].reshape(GROUP, 8)
        picked = [None, None]
        for e in range(EXPERTS):
            both = jnp.dot(block, wcat[:, 256 * e : 256 * (e + 1)], preferred_element_type=F32)
            for k in range(2):
                picked[k] = both if e == 0 else jnp.where(ids[:, k : k + 1] == float(e), both, picked[k])
        return picked

    def for_pair(d):
        for k, value in enumerate(terms(pair, d)):
            core_out[d, :, 256 * k : 256 * (k + 1)] = value
        send(core_out.at[d], core_in.at[d], ("c", d), {C: pair})

    def for_lanes(d):
        picked = terms(c, d)
        arrived(core_in.at[d], ("c", d))
        for k, value in enumerate(picked):
            cols = slice(256 * k, 256 * (k + 1))
            value = (value + core_in[d, :, cols]).reshape(4, PIECE, 256)
            own[d, :, :, cols] = value
            lane_out[d, :, :, cols] = value.astype(BF16)
        for j in (2, 3, 1):
            i = at(l, j)
            send(lane_out.at[d, i], lane_in.at[d, j - 1], ("l", d, j), {L: i})

    def hidden(d):
        o = at(outer_place(c), d)
        for j in (1, 3, 2):
            arrived(lane_in.at[d, j - 1], ("l", d, j))
        for k in range(2):
            cols = slice(256 * k, 256 * (k + 1))
            sums = own[d, l, :, cols]
            for j in range(3):
                sums = sums + lane_in[d, j, :, cols].astype(F32)
            gate, up = sums[:, :128], sums[:, 128:]
            weight = meta[c, o, l][:, 2 + k : 3 + k]
            hid[c, o, l, :, 128 * k : 128 * (k + 1)] = (gate / (1.0 + jnp.exp(-gate)) * up * weight).astype(BF16)
        mine = hid.at[c, o, l]
        for j in (2, 3, 1):
            send(mine, mine, ("h", d, j), step(L, j))
        send(mine, mine, ("p", d, 0), {C: pair})

    def forward(d):
        o = at(outer_place(c), d)
        for j in (1, 3, 2):
            piece = hid.at[c, o, at(l, 4 - j)]
            arrived(piece, ("h", d, j))
            send(piece, piece, ("p", d, j), {C: pair})

    def second(r, d, name):
        o = at(outer_place(r), d)
        if name == "pair":
            for j in range(4):
                arrived(hid.at[r, o, at(l, 4 - j)], ("p", d, j))
        ids = meta[r, o].reshape(GROUP, 8)
        units = hid[r, o].astype(F32).reshape(GROUP, 256)
        one, two = units[:, 0:128], units[:, 128:256]
        spread = []
        for e in range(EXPERTS):
            here = jnp.where(ids[:, 1:2] == float(e), two, 0.0)
            spread.append(jnp.where(ids[:, 0:1] == float(e), one, here).astype(BF16))
        spread = jnp.concatenate(spread, axis=1)
        result = jnp.dot(spread, wdown[...], preferred_element_type=F32).reshape(4, PIECE, WIDTH)
        if d == 0:
            part[r] = result
        else:
            send_part[r, d - 1] = result.astype(BF16)
            if d == 2:
                for k in (1, 3, 2, 0):
                    i = at(inner_place(r), k)
                    send(send_part.at[r, 1, i], in1.at[r, 1, i], ("s", name, d, k), outer_to(r, o))
            else:
                send(send_part.at[r, d - 1], in1.at[r, d - 1], ("s", name, d), outer_to(r, o))

    for_pair(0)
    pass_on(0)
    pass_on(3)
    for_lanes(0)
    pass_on(1)
    pass_on(2)
    for_pair(1)
    for_pair(3)
    for_lanes(1)
    for_lanes(3)
    hidden(0)
    opposite_arrived()
    for_pair(2)
    hidden(1)
    for_lanes(2)
    hidden(3)
    forward(1)
    second(c, 1, "own")
    hidden(2)
    forward(3)
    second(pair, 1, "pair")
    second(c, 3, "own")
    forward(2)
    second(pair, 3, "pair")
    second(c, 2, "own")
    second(pair, 2, "pair")
    forward(0)
    second(c, 0, "own")
    second(pair, 0, "pair")

    for name, r in (("own", c), ("pair", pair)):
        for d in (1, 3):
            arrived(in1.at[r, d - 1], ("s", name, d))
        for k in (1, 3, 2, 0):
            i = at(inner_place(r), k)
            arrived(in1.at[r, 1, i], ("s", name, 2, k))
            value = part[r, i]
            for d in range(3):
                value = value + in1[r, d, i].astype(F32)
            if k == 0:
                total[r] = value
            else:
                send_total[r, i] = value.astype(BF16)
                send(send_total.at[r, i], in2.at[r, k - 1], ("S", name, k), inner_to(r, i))
    from_zh = [number(("Z", d)) for d in range(4)][0]
    z_sends = []
    for name, r in (("own", c), ("pair", pair)):
        for d in (1, 3, 2):
            arrived(in2.at[r, d - 1], ("S", name, d))
        value = total[r]
        for d in range(3):
            value = value + in2[r, d].astype(F32)
        for zi in range(2):
            i = 2 * r + zi
            block = value[20 * zi : 20 * (zi + 1)]
            z_own[i] = block
            z_out[i] = pack(block)
            one = pltpu.make_async_remote_copy(
                src_ref=z_out.at[i], dst_ref=z_in.at[h], send_sem=ss.at[number(("Z", name, zi))],
                recv_sem=rs.at[from_zh + h], device_id={H: i}, device_id_type=MESH,
            )
            z_sends.append((i, one))
            pl.when(i != h)(one.start)
    for d in (1, 3, 2):
        arrived(z_in.at[at(h, d)], from_zh + at(h, d))
    value = z_in[at(h, 1)].astype(F32) + z_in[at(h, 2)].astype(F32) + z_in[at(h, 3)].astype(F32)
    mine = z_own[h]
    bottom = jnp.concatenate([value[4 * j : 4 * j + 4, WIDTH:] for j in range(3)], axis=1)
    out_ref[...] = (mine + jnp.concatenate([value[:, :WIDTH], bottom], axis=0)).astype(BF16)

    for one in sent:
        one.wait_send()
    for i, one in z_sends:
        pl.when(i != h)(one.wait_send)


def local(tokens, route_ids, route_probs, w_gate, w_up, w_down):
    hbm = pl.BlockSpec(memory_space=pl.ANY)
    return pl.pallas_call(
        kernel,
        out_shape=jax.ShapeDtypeStruct((20, WIDTH), BF16),
        in_specs=[hbm] * 6,
        out_specs=pl.BlockSpec(memory_space=pltpu.VMEM),
        scratch_shapes=[
            pltpu.VMEM((20, WIDTH), BF16),
            pltpu.VMEM((2, 1280), jnp.int32),
            pltpu.VMEM((2, 1280), BF16),
            pltpu.VMEM((WIDTH, 1024), BF16),
            pltpu.VMEM((512, WIDTH), BF16),
            pltpu.VMEM((2, 4, 4, PIECE, 8), F32),
            pltpu.VMEM((4, 16, 1024), BF16),
            pltpu.VMEM((80, WIDTH), F32),
            pltpu.VMEM((2, 4, 4, PIECE, WIDTH), BF16),
            pltpu.VMEM((4, GROUP, 512), F32),
            pltpu.VMEM((4, GROUP, 512), F32),
            pltpu.VMEM((4, 4, PIECE, 512), F32),
            pltpu.VMEM((4, 4, PIECE, 512), BF16),
            pltpu.VMEM((4, 3, PIECE, 512), BF16),
            pltpu.VMEM((2, 4, 4, PIECE, 256), BF16),
            pltpu.VMEM((2, 4, PIECE, WIDTH), F32),
            pltpu.VMEM((2, 3, 4, PIECE, WIDTH), BF16),
            pltpu.VMEM((2, 3, 4, PIECE, WIDTH), BF16),
            pltpu.VMEM((2, PIECE, WIDTH), F32),
            pltpu.VMEM((2, 4, PIECE, WIDTH), BF16),
            pltpu.VMEM((2, 3, PIECE, WIDTH), BF16),
            pltpu.VMEM((4, 20, WIDTH), F32),
            pltpu.VMEM((4, 16, 1024), BF16),
            pltpu.VMEM((4, 16, 1024), BF16),
            pltpu.SemaphoreType.DMA((15,)),
            pltpu.SemaphoreType.DMA((120,)),
            pltpu.SemaphoreType.DMA((120,)),
        ],
        compiler_params=pltpu.CompilerParams(
            collective_id=0, has_side_effects=True, vmem_limit_bytes=60 * 2**20
        ),
    )(tokens, route_ids.T, route_probs.T, w_gate, w_up, w_down)


def solution(mesh):
    torus = Mesh(mesh.devices.reshape(4, 4, 4, 4, 2), (X, H, Y, L, C))
    in_specs = (
        P(DP, TENSOR),
        P(),
        P(),
        P(None, TENSOR, DP),
        P(None, TENSOR, DP),
        P(None, DP, TENSOR),
    )
    return jax.shard_map(local, mesh=torus, in_specs=in_specs, out_specs=P(DP, TENSOR), check_vma=False)
```

```python
import jax
import jax.numpy as jnp
from jax import lax
from jax.experimental import pallas as pl
from jax.experimental.pallas import tpu as pltpu
from jax.sharding import Mesh
from jax.sharding import PartitionSpec as P

MESH = pl.DeviceIdType.MESH
F32, BF16 = jnp.float32, jnp.bfloat16
X, H, Y, L, C = "x", "zh", "y", "zl", "c"
DP = (X, H, Y)
TENSOR = (L, C)
EXPERTS = 4
WIDTH = 768
PIECE = 40
GROUP = 160


def kernel(
    tok_hbm, ids_hbm, probs_hbm, wg_ref, wu_ref, wd_ref, out_ref,
    tok_in, ids_in, probs_in, wcat, wdown, meta, packed, unpacked, tok,
    core_out, core_in, own, lane_out, lane_in, hid,
    part, send_part, in1, total, send_total, in2, z_own, z_out, z_in,
    w_sem, ss, rs,
):
    x, h, y, l, c = (lax.axis_index(a) for a in (X, H, Y, L, C))
    place = {X: x, H: h, Y: y, L: l, C: c}
    pair = 1 - c

    small = [(tok_hbm, tok_in), (ids_hbm, ids_in), (probs_hbm, probs_in)]
    loads = []
    for e in range(EXPERTS):
        loads.append((wg_ref.at[e], wcat.at[:, pl.ds(e * 256, 128)]))
        loads.append((wu_ref.at[e], wcat.at[:, pl.ds(e * 256 + 128, 128)]))
    for e in range(EXPERTS):
        loads.append((wd_ref.at[e], wdown.at[pl.ds(e * 128, 128), :]))
    loads = [pltpu.make_async_copy(s, d, w_sem.at[i]) for i, (s, d) in enumerate(small + loads)]
    for load in loads:
        load.start()

    def step(axis, by):
        return {axis: lax.rem(place[axis] + by, 4)}

    barrier = pltpu.get_barrier_semaphore()
    partners = [step(a, by) for a in (X, Y, H, L) for by in (1, 2, 3)] + [{C: pair}]
    for other in partners:
        pl.semaphore_signal(barrier, inc=1, device_id=other, device_id_type=MESH)

    sent, numbers = [], {}

    def number(key):
        return numbers.setdefault(key, len(numbers))

    def copy(src, dst, key, to):
        i = number(key) if isinstance(key, tuple) else key
        return pltpu.make_async_remote_copy(
            src_ref=src, dst_ref=dst, send_sem=ss.at[i], recv_sem=rs.at[i],
            device_id=to, device_id_type=MESH,
        )

    def send(src, dst, key, to):
        one = copy(src, dst, key, to)
        one.start()
        sent.append(one)

    def arrived(dst, key):
        copy(dst, dst, key, {C: pair}).wait_recv()

    def outer_place(r):
        return y + r * (x - y)

    def inner_place(r):
        return x + r * (y - x)

    def outer_to(r, o):
        return {X: x + r * (o - x), Y: o + r * (y - o)}

    def inner_to(r, i):
        return {X: i + r * (x - i), Y: y + r * (i - y)}

    def at(place_, d):
        return lax.rem(place_ + d, 4)

    for load in loads[:3]:
        load.wait()
    def pack(block):
        tail = [block[16:20, 256 * j : 256 * (j + 1)] for j in range(3)]
        tail = jnp.concatenate([*tail, jnp.zeros((4, 256), F32)], axis=0)
        return jnp.concatenate([block[0:16], tail], axis=1).astype(BF16)

    packed[h] = pack(tok_in[...].astype(F32))
    pl.semaphore_wait(barrier, len(partners))

    for d in (1, 2, 3):
        send(packed.at[h], packed.at[h], ("z", d), step(H, d))
    row = lax.broadcasted_iota(jnp.int32, (640, 1), 0)

    def count(value, size, most):
        return sum((value >= size * k).astype(jnp.int32) for k in range(1, most))

    xb = count(row, 320, 2)
    rest = row - 320 * xb
    part_of = count(rest, 160, 2)
    rest = rest - 160 * part_of
    yy = count(rest, PIECE, 4)
    rest = rest - PIECE * yy
    zz = count(rest, 20, 2)
    source = 320 * xb + (2 * part_of + zz) * 80 + yy * 20 + rest - 20 * zz
    order = (lax.broadcasted_iota(jnp.int32, (640, 640), 1) == source).astype(F32).astype(BF16)
    lines = jnp.concatenate([ids_in[...].astype(F32), probs_in[...].astype(F32), jnp.zeros((4, 1280), F32)], axis=0)
    lines = lines.astype(BF16)
    for two in range(2):
        columns = lax.dot_general(
            order, lines[:, 640 * two : 640 * (two + 1)], (((1,), (1,)), ((), ())), preferred_element_type=F32
        )
        for one in range(2):
            for yi in range(4):
                xi = 2 * two + one
                at0 = 320 * one + PIECE * yi
                meta[0, yi, xi] = columns[at0 : at0 + PIECE]
                meta[1, xi, yi] = columns[at0 + 160 : at0 + 160 + PIECE]

    for d in (1, 3, 2):
        arrived(packed.at[at(h, 4 - d)], ("z", d))
    for i in range(4):
        block = packed[i].astype(F32)
        unpacked[20 * i : 20 * i + 16] = block[:, 0:WIDTH]
        for j in range(3):
            unpacked[20 * i + 16 : 20 * i + 20, 256 * j : 256 * (j + 1)] = block[4 * j : 4 * j + 4, WIDTH:]
    def share_block(r, d, k):
        mine = tok.at[r, outer_place(r), at(inner_place(r), k)]
        send(mine, mine, ("T", r, d, k), outer_to(r, at(outer_place(r), d)))

    def pass_on(k):
        for r in range(2):
            for d, blocks in ((3, (0, 1)), (1, (3, 2))):
                block = tok.at[r, at(outer_place(r), d), at(inner_place(r), k)]
                arrived(block, ("T", r, 4 - d, k))
                if k in blocks:
                    send(block, block, ("T", r, 2, k), outer_to(r, at(outer_place(r), 4 - d)))

    def opposite_arrived():
        for r in range(2):
            for k in range(4):
                arrived(tok.at[r, at(outer_place(r), 2), at(inner_place(r), k)], ("T", r, 2, k))

    for r in range(2):
        mine = tok.at[r, outer_place(r), inner_place(r)]
        mine[...] = unpacked[PIECE * r : PIECE * (r + 1)].astype(BF16)
        for d in (1, 3, 2):
            send(mine, mine, ("t", r, d), inner_to(r, at(inner_place(r), d)))
    for r in range(2):
        share_block(r, 1, 0)
        share_block(r, 3, 0)
    for d in (1, 3, 2):
        for r in range(2):
            arrived(tok.at[r, outer_place(r), at(inner_place(r), 4 - d)], ("t", r, d))
            share_block(r, 1, 4 - d)
            share_block(r, 3, 4 - d)
    for load in loads[3:]:
        load.wait()

    def terms(r, d):
        o = at(outer_place(r), d)
        block = tok[r, o].astype(F32).reshape(GROUP, WIDTH).astype(BF16)
        ids = meta[r, o].reshape(GROUP, 8)
        picked = [None, None]
        for e in range(EXPERTS):
            both = jnp.dot(block, wcat[:, 256 * e : 256 * (e + 1)], preferred_element_type=F32)
            for k in range(2):
                picked[k] = both if e == 0 else jnp.where(ids[:, k : k + 1] == float(e), both, picked[k])
        return picked

    def for_pair(d):
        for k, value in enumerate(terms(pair, d)):
            core_out[d, :, 256 * k : 256 * (k + 1)] = value
        send(core_out.at[d], core_in.at[d], ("c", d), {C: pair})

    def for_lanes(d):
        picked = terms(c, d)
        arrived(core_in.at[d], ("c", d))
        for k, value in enumerate(picked):
            cols = slice(256 * k, 256 * (k + 1))
            value = (value + core_in[d, :, cols]).reshape(4, PIECE, 256)
            own[d, :, :, cols] = value
            lane_out[d, :, :, cols] = value.astype(BF16)
        for j in (2, 3, 1):
            i = at(l, j)
            send(lane_out.at[d, i], lane_in.at[d, j - 1], ("l", d, j), {L: i})

    def hidden(d):
        o = at(outer_place(c), d)
        for j in (1, 3, 2):
            arrived(lane_in.at[d, j - 1], ("l", d, j))
        for k in range(2):
            cols = slice(256 * k, 256 * (k + 1))
            sums = own[d, l, :, cols]
            for j in range(3):
                sums = sums + lane_in[d, j, :, cols].astype(F32)
            gate, up = sums[:, :128], sums[:, 128:]
            weight = meta[c, o, l][:, 2 + k : 3 + k]
            hid[c, o, l, :, 128 * k : 128 * (k + 1)] = (gate / (1.0 + jnp.exp(-gate)) * up * weight).astype(BF16)
        mine = hid.at[c, o, l]
        for j in (2, 3, 1):
            send(mine, mine, ("h", d, j), step(L, j))
        send(mine, mine, ("p", d, 0), {C: pair})

    def forward(d):
        o = at(outer_place(c), d)
        for j in (1, 3, 2):
            piece = hid.at[c, o, at(l, 4 - j)]
            arrived(piece, ("h", d, j))
            send(piece, piece, ("p", d, j), {C: pair})

    def second(r, d, name):
        o = at(outer_place(r), d)
        if name == "pair":
            for j in range(4):
                arrived(hid.at[r, o, at(l, 4 - j)], ("p", d, j))
        ids = meta[r, o].reshape(GROUP, 8)
        units = hid[r, o].astype(F32).reshape(GROUP, 256)
        one, two = units[:, 0:128], units[:, 128:256]
        spread = []
        for e in range(EXPERTS):
            here = jnp.where(ids[:, 1:2] == float(e), two, 0.0)
            spread.append(jnp.where(ids[:, 0:1] == float(e), one, here).astype(BF16))
        spread = jnp.concatenate(spread, axis=1)
        result = jnp.dot(spread, wdown[...], preferred_element_type=F32).reshape(4, PIECE, WIDTH)
        if d == 0:
            part[r] = result
        else:
            send_part[r, d - 1] = result.astype(BF16)
            if d == 2:
                for k in (1, 3, 2, 0):
                    i = at(inner_place(r), k)
                    send(send_part.at[r, 1, i], in1.at[r, 1, i], ("s", name, d, k), outer_to(r, o))
            else:
                send(send_part.at[r, d - 1], in1.at[r, d - 1], ("s", name, d), outer_to(r, o))

    for_pair(0)
    pass_on(0)
    pass_on(3)
    for_lanes(0)
    pass_on(1)
    pass_on(2)
    for_pair(1)
    for_pair(3)
    for_lanes(1)
    for_lanes(3)
    opposite_arrived()
    for_pair(2)
    hidden(1)
    for_lanes(2)
    hidden(3)
    forward(1)
    second(c, 1, "own")
    hidden(2)
    forward(3)
    second(pair, 1, "pair")
    second(c, 3, "own")
    forward(2)
    hidden(0)
    second(pair, 3, "pair")
    second(c, 2, "own")
    second(pair, 2, "pair")
    forward(0)
    second(c, 0, "own")
    second(pair, 0, "pair")

    for name, r in (("own", c), ("pair", pair)):
        for d in (1, 3):
            arrived(in1.at[r, d - 1], ("s", name, d))
        for k in (1, 3, 2, 0):
            i = at(inner_place(r), k)
            arrived(in1.at[r, 1, i], ("s", name, 2, k))
            value = part[r, i]
            for d in range(3):
                value = value + in1[r, d, i].astype(F32)
            if k == 0:
                total[r] = value
            else:
                send_total[r, i] = value.astype(BF16)
                send(send_total.at[r, i], in2.at[r, k - 1], ("S", name, k), inner_to(r, i))
    from_zh = [number(("Z", d)) for d in range(4)][0]
    z_sends = []
    for name, r in (("own", c), ("pair", pair)):
        for d in (1, 3, 2):
            arrived(in2.at[r, d - 1], ("S", name, d))
        value = total[r]
        for d in range(3):
            value = value + in2[r, d].astype(F32)
        for zi in range(2):
            i = 2 * r + zi
            block = value[20 * zi : 20 * (zi + 1)]
            z_own[i] = block
            z_out[i] = pack(block)
            one = pltpu.make_async_remote_copy(
                src_ref=z_out.at[i], dst_ref=z_in.at[h], send_sem=ss.at[number(("Z", name, zi))],
                recv_sem=rs.at[from_zh + h], device_id={H: i}, device_id_type=MESH,
            )
            z_sends.append((i, one))
            pl.when(i != h)(one.start)
    for d in (1, 3, 2):
        arrived(z_in.at[at(h, d)], from_zh + at(h, d))
    value = z_in[at(h, 1)].astype(F32) + z_in[at(h, 2)].astype(F32) + z_in[at(h, 3)].astype(F32)
    mine = z_own[h]
    bottom = jnp.concatenate([value[4 * j : 4 * j + 4, WIDTH:] for j in range(3)], axis=1)
    out_ref[...] = (mine + jnp.concatenate([value[:, :WIDTH], bottom], axis=0)).astype(BF16)

    for one in sent:
        one.wait_send()
    for i, one in z_sends:
        pl.when(i != h)(one.wait_send)


def local(tokens, route_ids, route_probs, w_gate, w_up, w_down):
    hbm = pl.BlockSpec(memory_space=pl.ANY)
    return pl.pallas_call(
        kernel,
        out_shape=jax.ShapeDtypeStruct((20, WIDTH), BF16),
        in_specs=[hbm] * 6,
        out_specs=pl.BlockSpec(memory_space=pltpu.VMEM),
        scratch_shapes=[
            pltpu.VMEM((20, WIDTH), BF16),
            pltpu.VMEM((2, 1280), jnp.int32),
            pltpu.VMEM((2, 1280), BF16),
            pltpu.VMEM((WIDTH, 1024), BF16),
            pltpu.VMEM((512, WIDTH), BF16),
            pltpu.VMEM((2, 4, 4, PIECE, 8), F32),
            pltpu.VMEM((4, 16, 1024), BF16),
            pltpu.VMEM((80, WIDTH), F32),
            pltpu.VMEM((2, 4, 4, PIECE, WIDTH), BF16),
            pltpu.VMEM((4, GROUP, 512), F32),
            pltpu.VMEM((4, GROUP, 512), F32),
            pltpu.VMEM((4, 4, PIECE, 512), F32),
            pltpu.VMEM((4, 4, PIECE, 512), BF16),
            pltpu.VMEM((4, 3, PIECE, 512), BF16),
            pltpu.VMEM((2, 4, 4, PIECE, 256), BF16),
            pltpu.VMEM((2, 4, PIECE, WIDTH), F32),
            pltpu.VMEM((2, 3, 4, PIECE, WIDTH), BF16),
            pltpu.VMEM((2, 3, 4, PIECE, WIDTH), BF16),
            pltpu.VMEM((2, PIECE, WIDTH), F32),
            pltpu.VMEM((2, 4, PIECE, WIDTH), BF16),
            pltpu.VMEM((2, 3, PIECE, WIDTH), BF16),
            pltpu.VMEM((4, 20, WIDTH), F32),
            pltpu.VMEM((4, 16, 1024), BF16),
            pltpu.VMEM((4, 16, 1024), BF16),
            pltpu.SemaphoreType.DMA((15,)),
            pltpu.SemaphoreType.DMA((120,)),
            pltpu.SemaphoreType.DMA((120,)),
        ],
        compiler_params=pltpu.CompilerParams(
            collective_id=0, has_side_effects=True, vmem_limit_bytes=60 * 2**20
        ),
    )(tokens, route_ids.T, route_probs.T, w_gate, w_up, w_down)


def solution(mesh):
    torus = Mesh(mesh.devices.reshape(4, 4, 4, 4, 2), (X, H, Y, L, C))
    in_specs = (
        P(DP, TENSOR),
        P(),
        P(),
        P(None, TENSOR, DP),
        P(None, TENSOR, DP),
        P(None, DP, TENSOR),
    )
    return jax.shard_map(local, mesh=torus, in_specs=in_specs, out_specs=P(DP, TENSOR), check_vma=False)
```
